256 devices in a mesh: cam: 16 (over z, core), pt: 16 (over y, x).
Axes of the slice: x: 4, y: 4, z: 8, core: 2. Of those that a mesh axis runs over, the one named last changes fastest.
Arguments:
- right_side: float32 [9, 65536], P(None, ('cam', 'pt')), may hold values from -6 to 6
- precond_diag: float32 [9, 65536], P(None, ('cam', 'pt')), may hold values from 0.1 to 0.5
- camera_damping: float32 [9, 65536], P(None, ('cam', 'pt')), may hold values from 0.1 to 1
- point_damping: float32 [3, 16, 4096], P(None, 'cam', 'pt'), may hold values from 0.1 to 1
- camera_jacobian: bfloat16 [16, 16, 18, 64, 128], P('cam', 'pt'), may hold values from -0.375 to 0.375
- point_jacobian: bfloat16 [16, 16, 6, 64, 128], P('cam', 'pt'), may hold values from -1.5 to 1.5
- camera_index: int32 [16, 16, 64, 128], P('cam', 'pt'), may hold values from 0 to 4095
- point_index: int32 [16, 16, 64, 128], P('cam', 'pt'), may hold values from 0 to 4095
- tile_count: int32 [16, 16], P('cam', 'pt'), may hold values from 1 to 64, 512 in all within a row
Outputs:
- solution: float32 [9, 65536], P(None, ('cam', 'pt'))
- residual: float32 [9, 65536], P(None, ('cam', 'pt'))
The draws below stay inside these ranges and needn't reach their ends.
Inputs may be any that keep to these rules, and one draw needn't show every extreme that they name: `tile_count`: for every index of cam the counts over pt sum to 512, and the largest of them is 64.
All inputs are finite; a program needn't handle non-finite values. No bound on the sum of `tile_count` on one device may be relied on, other than what follows from the above.
Results may differ from the reference program's by a relative error of at most 0.0003.
Values sent between devices are 32-bit elements; how exact they have to be, the bound alone decides.
A program may use at most 64 MiB of HBM per device.

```python
import math
import jax
import jax.numpy as jnp
import numpy as np
from jax import lax

CAM_DEV = 256
TILES_DEV = 64
ITERS = 3
PT_DEV = 256
CAM_BLK = 4096
CAMERAS = 65536
PT_BLK = 4096
PT_ROW = 4096
N_CAM = 16
N_PT = 16


def touch_ends(values, stream_key, least, largest):
    spot = [jax.random.randint(jax.random.fold_in(stream_key, axis), (), 0, length) for axis, length in enumerate(values.shape)]
    longest = values.shape.index(max(values.shape))
    next_to = spot[:longest] + [(spot[longest] + 1) % values.shape[longest]] + spot[longest + 1:]
    return values.at[tuple(spot)].set(least).at[tuple(next_to)].set(largest)


def shard_levels(own_key, shape, split, least, largest):
    factor_of, own = 1.0, jax.random.fold_in(own_key, 6)
    for axis_at, blocks in split:
        heights = jnp.exp(jax.random.uniform(jax.random.fold_in(own, axis_at), (blocks,), jnp.float32, least / len(split), largest / len(split)))
        factor_of = factor_of * jnp.repeat(heights, shape[axis_at] // blocks).reshape([-1 if axis == axis_at else 1 for axis in range(len(shape))])
    return factor_of


def profile(number_of, total, most, slope):
    portions = [(1 << 20) // math.isqrt(grade ** slope) + 1 for grade in range(2, number_of + 1)]
    spare, given = total - most - (number_of - 1), [1] * (number_of - 1)
    while spare > 0:
        free = [i for i in range(number_of - 1) if given[i] < most]
        whole, budget = sum([portions[i] for i in free]), spare
        for i in free:
            extra = min(most - given[i], max(1, budget * portions[i] // whole), spare)
            given[i] = given[i] + extra
            spare = spare - extra
    return np.array([most] + given)


def ragged(rng, number_of, total, bound, lean):
    if number_of == 2:
        one = jax.random.randint(rng, (), max(1, total - bound), min(bound, total - 1) + 1)
        return jnp.stack([one, total - one])
    sizes = jnp.asarray(profile(number_of, total, bound, lean), jnp.int32)
    twos = (number_of - 1) // 2
    donor, taker = sizes[1:1 + 2 * twos:2], sizes[2:2 + 2 * twos:2]
    margin = jnp.minimum(donor - 1, bound - taker)
    moved = jax.random.randint(jax.random.fold_in(rng, 1), (twos,), 0, 1 << 20) % (margin + 1)
    sizes = sizes.at[1:1 + 2 * twos:2].set(donor - moved).at[2:2 + 2 * twos:2].set(taker + moved)
    return sizes[jax.random.permutation(jax.random.fold_in(rng, 2), number_of)]


def bell_draw(own_key, shape, scale, reach, cuts=(), held_as=jnp.bfloat16):
    loudness = shard_levels(own_key, shape, cuts, -0.22, 0.18) if cuts else 1.0
    entries = jax.random.normal(own_key, shape, jnp.float32) * scale * loudness
    return jnp.minimum(jnp.maximum(entries, -reach), reach).astype(held_as)


def setup_inputs(seed: int = 0) -> dict:
    splits = jax.random.split(jax.random.key(seed), 10)
    return {
        "right_side": bell_draw(splits[0], (9, CAMERAS), 1.0, 6.0, ((1, 256),), jnp.float32),
        "precond_diag": jnp.clip(jnp.exp(math.log(0.5) - 1.609438 * jax.random.uniform(splits[1], (9, CAMERAS), jnp.float32) ** shard_levels(splits[1], (9, CAMERAS), ((1, 256),), -0.2, 0.2)), 0.1, 0.5),
        "camera_damping": jnp.clip(jnp.exp(math.log(1.0) - 2.3025851 * jax.random.uniform(splits[2], (9, CAMERAS), jnp.float32) ** shard_levels(splits[2], (9, CAMERAS), ((1, 256),), -0.2, 0.2)), 0.1, 1.0),
        "point_damping": jnp.clip(jnp.exp(math.log(1.0) - 2.3025851 * jax.random.uniform(splits[3], (3, N_CAM, PT_ROW), jnp.float32) ** shard_levels(splits[3], (3, N_CAM, PT_ROW), ((1, 16), (2, 16)), -0.2, 0.2)), 0.1, 1.0),
        "camera_jacobian": bell_draw(splits[4], (N_CAM, N_PT, 18, TILES_DEV, 128), 0.0625, 0.375, ((0, 16), (1, 16))),
        "point_jacobian": bell_draw(splits[5], (N_CAM, N_PT, 6, TILES_DEV, 128), 0.25, 1.5, ((0, 16), (1, 16))),
        "camera_index": touch_ends(jax.random.randint(splits[6], (N_CAM, N_PT, TILES_DEV, 128), 0, CAM_BLK), jax.random.fold_in(splits[6], 1), 0, CAM_BLK - 1).astype(jnp.int32),
        "point_index": touch_ends(jax.random.randint(splits[7], (N_CAM, N_PT, TILES_DEV, 128), 0, PT_BLK), jax.random.fold_in(splits[7], 1), 0, PT_BLK - 1).astype(jnp.int32),
        "tile_count": jax.vmap(lambda own: ragged(own, N_PT, N_PT * TILES_DEV // 2, TILES_DEV, 2))(jax.random.split(splits[8], N_CAM)).reshape((N_CAM, N_PT)).astype(jnp.int32),
    }


sym_pairs = ((0, 0), (0, 1), (0, 2), (1, 1), (1, 2), (2, 2))
sym_lookup = ((0, 1, 2), (1, 3, 4), (2, 4, 5))


def curvature_terms(jac_point):
    return jnp.stack([jac_point[left_idx] * jac_point[right_idx] + jac_point[3 + left_idx] * jac_point[3 + right_idx] for left_idx, right_idx in sym_pairs])


def invert_blocks(hess):
    top_left, top_mid, top_right, mid_mid, mid_right, low_right = hess[0], hess[1], hess[2], hess[3], hess[4], hess[5]
    adj_one = mid_mid * low_right - mid_right * mid_right
    adj_two = top_right * mid_right - top_mid * low_right
    adj_three = top_mid * mid_right - top_right * mid_mid
    adj_four = top_left * low_right - top_right * top_right
    adj_five = top_mid * top_right - top_left * mid_right
    adj_six = top_left * mid_mid - top_mid * top_mid
    determ = top_left * adj_one + top_mid * adj_two + top_right * adj_three
    return jnp.stack([adj_one, adj_two, adj_three, adj_four, adj_five, adj_six]) / determ


def apply_blocks(inverse, vector):
    return jnp.stack([sum(inverse[sym_lookup[row_id][column]] * vector[column] for column in range(3)) for row_id in range(3)])


def camera_response(jac_camera, gathered):
    return jnp.stack([jnp.sum(jac_camera[:9] * gathered, axis=0), jnp.sum(jac_camera[9:] * gathered, axis=0)])


def point_terms(jac_point, response):
    return jnp.stack([jac_point[column] * response[0] + jac_point[3 + column] * response[1] for column in range(3)])


def point_apply(jac_point, values):
    return jnp.stack([sum(jac_point[3 * row_id + column] * values[column] for column in range(3)) for row_id in range(2)])


def camera_terms(jac_camera, weight):
    return jnp.stack([jac_camera[column] * weight[0] + jac_camera[9 + column] * weight[1] for column in range(9)])


def reference(right_side, precond_diag, camera_damping, point_damping, camera_jacobian, point_jacobian, camera_index, point_index, tile_count):
    live = jnp.arange(TILES_DEV, dtype=jnp.int32)[None, None, :] < tile_count[:, :, None]
    live_mask = live[:, :, None, :, None]
    zero_half = jnp.zeros((), jnp.bfloat16)
    jac_cam = jnp.where(live_mask, camera_jacobian, zero_half)
    jac_pnt = jnp.where(live_mask, point_jacobian, zero_half)
    obs_rows = N_PT * TILES_DEV * 128

    def flatten(array):
        return jnp.moveaxis(array, 2, 1).reshape(array.shape[0], array.shape[2], obs_rows)

    cam_flat = flatten(jac_cam)
    pnt_flat = flatten(jac_pnt)
    cam_offset = (jnp.arange(N_CAM, dtype=jnp.int32) * (CAM_DEV * N_PT))[:, None, None, None]
    cam_global = (camera_index + cam_offset).reshape(N_CAM, obs_rows)
    column_off = (jnp.arange(N_PT, dtype=jnp.int32) * PT_DEV)[None, :, None, None]
    pnt_global = ((point_index // PT_DEV) * (N_PT * PT_DEV) + column_off + point_index % PT_DEV).reshape(N_CAM, obs_rows)
    all_points = N_CAM * N_PT * PT_DEV
    damping = point_damping.reshape(3, all_points)

    def hess_row(total, inputs):
        jac_point, point_ids = inputs
        return total.at[:, point_ids].add(curvature_terms(jac_point.astype(jnp.float32))), None

    hess, unused = lax.scan(hess_row, jnp.zeros((6, all_points), jnp.float32), (pnt_flat, pnt_global))
    zero_pts = jnp.zeros((all_points,), jnp.float32)
    hess = hess + jnp.stack([damping[0], zero_pts, zero_pts, damping[1], zero_pts, damping[2]])
    inverse = invert_blocks(hess)

    def schur_apply(vector):
        def point_row(total, inputs):
            jac_camera, jac_point, cam_ids, point_ids = inputs
            response = camera_response(jac_camera, vector[:, cam_ids])
            return total.at[:, point_ids].add(point_terms(jac_point, response)), None

        point_sum, unused_one = lax.scan(point_row, jnp.zeros((3, all_points), jnp.float32), (cam_flat, pnt_flat, cam_global, pnt_global))
        solved = apply_blocks(inverse, point_sum)

        def camera_row(total, inputs):
            jac_camera, jac_point, cam_ids, point_ids = inputs
            response = camera_response(jac_camera, vector[:, cam_ids])
            weight = response - point_apply(jac_point, solved[:, point_ids])
            return total.at[:, cam_ids].add(camera_terms(jac_camera, weight)), None

        cam_sum, unused_two = lax.scan(camera_row, jnp.zeros(vector.shape, jnp.float32), (cam_flat, pnt_flat, cam_global, pnt_global))
        return cam_sum + camera_damping * vector

    solution = jnp.zeros_like(right_side)
    residual = right_side
    scaled = precond_diag * residual
    direction = scaled
    energy = jnp.sum(residual * scaled)
    for iteration in range(ITERS):
        image = schur_apply(direction)
        step_len = energy / jnp.sum(direction * image)
        solution = solution + step_len * direction
        residual = residual - step_len * image
        scaled = precond_diag * residual
        energy_next = jnp.sum(residual * scaled)
        direction = scaled + (energy_next / energy) * direction
        energy = energy_next
    return solution, residual
```

```python
import functools

import jax
import jax.numpy as jnp
from jax import lax
from jax.experimental import pallas as pl
from jax.experimental.pallas import tpu as pltpu
from jax.sharding import PartitionSpec as P

ITERS = 3
MESH = pl.DeviceIdType.MESH
f32, bf16, i32 = jnp.float32, jnp.bfloat16, jnp.int32

HI = 16
LO = 256
PAIRS = ((0, 0), (0, 1), (0, 2), (1, 1), (1, 2), (2, 2))
SYM = ((0, 1, 2), (1, 3, 4), (2, 4, 5))
GRP = 8


def kernel(
    n_cam, n_pt, tiles,
    rhs, pre, damp, pdamp, jc, jp, cidx, pidx, tcount,
    x_out, r_out,
    ohc, ohp, jcf, jpf, tab_hi, tab_lo, term, amat, acc,
    u_z, u_d, w_s,
    prec_s, damp_s, x_s, r_s, d_s, pz_s, inv_s, gam_s,
    buf_a, msg_b, buf_b, buf_c, buf_s, msg_d, buf_d, msg_h, buf_h,
    sa, ra, sb, rb, sc, rc, ss, rs, sd, rd, sh, rh,
):
    ci = lax.axis_index("cam")
    pi = lax.axis_index("pt")

    def cam_peer(step):
        return lax.rem(ci + step, n_cam)

    def pt_peer(step):
        return lax.rem(pi + step, n_pt)

    def cam_id(peer):
        return (peer, pi)

    def pt_id(peer):
        return (ci, peer)

    def send_all(ways, peer_of, id_of, src_of, dst, send_sem, recv_sem, me):
        def one(step, carry):
            peer = peer_of(step)
            pltpu.make_async_remote_copy(
                src_ref=src_of(peer), dst_ref=dst.at[me],
                send_sem=send_sem.at[peer], recv_sem=recv_sem.at[me],
                device_id=id_of(peer), device_id_type=MESH,
            ).start()
            return carry

        lax.fori_loop(1, ways, one, 0)

    def wait_all(ways, peer_of, id_of, src_of, dst, send_sem, recv_sem, me, sent):
        def one(step, carry):
            peer = peer_of(step)
            copy = pltpu.make_async_remote_copy(
                src_ref=src_of(peer), dst_ref=dst.at[peer],
                send_sem=send_sem.at[peer], recv_sem=recv_sem.at[peer],
                device_id=id_of(peer), device_id_type=MESH,
            )
            if sent:
                copy.wait_send()
            else:
                copy.wait_recv()
            return carry

        lax.fori_loop(1, ways, one, 0)

    ex_a = (n_pt, pt_peer, pt_id, lambda peer: buf_a.at[pi], buf_a, sa, ra, pi)
    ex_b = (n_cam, cam_peer, cam_id, lambda peer: msg_b.at[peer], buf_b, sb, rb, ci)
    ex_c = (n_cam, cam_peer, cam_id, lambda peer: buf_c.at[ci], buf_c, sc, rc, ci)
    ex_s = (n_cam, cam_peer, cam_id, lambda peer: buf_s.at[ci], buf_s, ss, rs, ci)
    ex_d = (n_pt, pt_peer, pt_id, lambda peer: msg_d.at[peer], buf_d, sd, rd, pi)
    ex_h = (n_cam, cam_peer, cam_id, lambda peer: msg_h.at[peer], buf_h, sh, rh, ci)

    barrier = pltpu.get_barrier_semaphore()

    def greet(ways, peer_of, id_of):
        def one(step, carry):
            pl.semaphore_signal(barrier, inc=1, device_id=id_of(peer_of(step)), device_id_type=MESH)
            return carry

        lax.fori_loop(1, ways, one, 0)

    greet(n_pt, pt_peer, pt_id)
    greet(n_cam, cam_peer, cam_id)

    def to_share(src, dst):
        dst[...] = jnp.zeros((24, 128), f32)
        dst[0:9, :] = src[:, 0:128]
        dst[9:18, :] = src[:, 128:256]

    to_share(rhs, r_s)
    to_share(pre, prec_s)
    to_share(damp, damp_s)
    x_s[...] = jnp.zeros((24, 128), f32)
    d_s[...] = jnp.zeros((24, 128), f32)
    pz_s[...] = jnp.zeros((8, 128), f32)
    u_d[...] = jnp.zeros_like(u_d)
    gam_s[...] = jnp.ones((1, 128), f32)

    def start_a():
        r = r_s[...]
        z = prec_s[...] * r
        g = jnp.sum(r * z, axis=0, keepdims=True)
        buf_a[pi] = z
        buf_a[pi, 18:19, :] = g
        return z

    live = lax.broadcasted_iota(i32, (tiles, 128), 0) < tcount[0, 0]
    for row in range(18):
        jcf[row] = jnp.where(live, jc[row].astype(f32), 0.0)
    for row in range(6):
        jpf[row] = jnp.where(live, jp[row].astype(f32), 0.0)
    low_iota = lax.broadcasted_iota(i32, (LO, 128), 0)

    def one_hot(idx, dst):
        def one(t, carry):
            low = jnp.broadcast_to(idx[pl.ds(t, 1), :] & (LO - 1), (LO, 128))
            dst[:, pl.ds(pl.multiple_of(t * 128, 128), 128)] = jnp.where(low == low_iota, 1.0, 0.0).astype(bf16)
            return carry

        lax.fori_loop(0, tiles, one, 0)

    one_hot(cidx, ohc)
    one_hot(pidx, ohp)

    hi_iota = lax.broadcasted_iota(i32, (HI, 128), 0)

    def hi_mask(idx, t):
        return jnp.broadcast_to(idx[pl.ds(t, 1), :] >> 8, (HI, 128)) == hi_iota

    def scatter(nk, idx, oh):
        rows = 2 * nk * HI
        acc[:, 0:rows, :] = jnp.zeros((2, rows, 128), f32)

        def step(c, carry):
            for s in range(GRP):
                t = c * GRP + s
                m = hi_mask(idx, t)
                for part in range(2):
                    for k in range(nk):
                        row = jnp.broadcast_to(term[part, k, pl.ds(t, 1), :], (HI, 128))
                        at = (part * nk + k) * HI
                        amat[at : at + HI, s * 128 : (s + 1) * 128] = jnp.where(m, row, 0.0).astype(bf16)
            cols = pl.ds(pl.multiple_of(c * (GRP * 128), GRP * 128), GRP * 128)
            res = lax.dot_general(
                amat[0:rows, :], oh[:, cols], (((1,), (1,)), ((), ())), preferred_element_type=f32
            )
            acc[0, 0:rows, :] += res[:, 0:128]
            acc[1, 0:rows, :] += res[:, 128:256]
            return carry

        lax.fori_loop(0, tiles // GRP, step, 0)

    def put_term(k, value):
        high = value.astype(bf16).astype(f32)
        term[0, k] = high
        term[1, k] = value - high

    def part_sum(nk, share, half):
        return (
            acc[half, pl.ds(share, nk, stride=HI), :]
            + acc[half, pl.ds(nk * HI + share, nk, stride=HI), :]
        )

    def gather(nk, table, idx, oh, jac, done):
        rows = nk * HI
        for k in range(nk):
            for half in range(2):
                val = table(k, half)
                high = val.astype(bf16)
                at, lanes = k * HI, slice(half * 128, half * 128 + 128)
                tab_hi[at : at + HI, lanes] = high
                tab_lo[at : at + HI, lanes] = (val - high.astype(f32)).astype(bf16)

        def step(c, carry):
            o = oh[:, pl.ds(pl.multiple_of(c * 256, 256), 256)]
            res = jnp.dot(tab_hi[0:rows, :], o, preferred_element_type=f32) + jnp.dot(
                tab_lo[0:rows, :], o, preferred_element_type=f32
            )
            for s in range(2):
                t = 2 * c + s
                m = hi_mask(idx, t)
                mine = res[:, s * 128 : (s + 1) * 128]
                for comp in range(2):
                    tot = sum(
                        mine[k * HI : k * HI + HI] * jac[comp * nk + k, pl.ds(t, 1), :] for k in range(nk)
                    )
                    done(comp, t, jnp.sum(jnp.where(m, tot, 0.0), axis=0, keepdims=True))
            return carry

        lax.fori_loop(0, tiles // 2, step, 0, unroll=4)

    start_a()
    pl.semaphore_wait(barrier, (n_pt - 1) + (n_cam - 1))
    send_all(*ex_a)

    for k, (a, b) in enumerate(PAIRS):
        put_term(k, jpf[a] * jpf[b] + jpf[3 + a] * jpf[3 + b])
    scatter(6, pidx, ohp)
    for share in range(n_cam):
        msg_h[share, 0:6, :] = part_sum(6, share, 0)
        msg_h[share, 8:14, :] = part_sum(6, share, 1)
        msg_h[share, 6:8, :] = jnp.zeros((2, 128), f32)
        msg_h[share, 14:16, :] = jnp.zeros((2, 128), f32)
    buf_h[ci] = msg_h[ci]
    send_all(*ex_h)

    def solve_curvature():
        wait_all(*ex_h, False)
        h = buf_h[0]
        for share in range(1, n_cam):
            h = h + buf_h[share]
        for half in range(2):
            lanes = slice(half * 128, half * 128 + 128)
            e = [h[8 * half + k : 8 * half + k + 1, :] for k in range(6)]
            e[0] = e[0] + pdamp[0:1, lanes]
            e[3] = e[3] + pdamp[1:2, lanes]
            e[5] = e[5] + pdamp[2:3, lanes]
            a1 = e[3] * e[5] - e[4] * e[4]
            a2 = e[2] * e[4] - e[1] * e[5]
            a3 = e[1] * e[4] - e[2] * e[3]
            a4 = e[0] * e[5] - e[2] * e[2]
            a5 = e[1] * e[2] - e[0] * e[4]
            a6 = e[0] * e[3] - e[1] * e[1]
            det = e[0] * a1 + e[1] * a2 + e[2] * a3
            for k, value in enumerate((a1, a2, a3, a4, a5, a6)):
                inv_s[8 * half + k : 8 * half + k + 1, :] = value / det
        wait_all(*ex_h, True)

    def iteration(it, carry):
        wait_all(*ex_a, False)
        grow = buf_a[0, 18:19, :]
        for share in range(1, n_pt):
            grow = grow + buf_a[share, 18:19, :]

        def put_u(comp, t, value):
            u_z[comp, pl.ds(t, 1), :] = value

        gather(9, lambda k, half: buf_a[:, 9 * half + k, :], cidx, ohc, jcf, put_u)

        u0, u1 = u_z[0], u_z[1]
        for k in range(3):
            put_term(k, jpf[k] * u0 + jpf[3 + k] * u1)
        scatter(3, pidx, ohp)
        for share in range(n_cam):
            msg_b[share, 0:3, :] = part_sum(3, share, 0)
            msg_b[share, 4:7, :] = part_sum(3, share, 1)
            msg_b[share, 3:4, :] = grow
            msg_b[share, 7:8, :] = jnp.zeros((1, 128), f32)
        buf_b[ci] = msg_b[ci]
        send_all(*ex_b)
        wait_all(*ex_a, True)

        @pl.when(it == 0)
        def _():
            solve_curvature()

        wait_all(*ex_b, False)
        pz = buf_b[0]
        for share in range(1, n_cam):
            pz = pz + buf_b[share]
        energy = jnp.broadcast_to(jnp.sum(pz[3:4, :], axis=1, keepdims=True), (1, 128))
        beta = jnp.where(it == 0, 0.0, energy / gam_s[...])
        gam_s[...] = energy
        pd = pz + beta * pz_s[...]
        pz_s[...] = pd
        for half in range(2):
            v = [pd[4 * half + k : 4 * half + k + 1, :] for k in range(3)]
            m = [inv_s[8 * half + k : 8 * half + k + 1, :] for k in range(6)]
            for row in range(3):
                at = 4 * half + row
                buf_c[ci, at : at + 1, :] = sum(m[SYM[row][col]] * v[col] for col in range(3))
            buf_c[ci, 4 * half + 3 : 4 * half + 4, :] = jnp.zeros((1, 128), f32)
        send_all(*ex_c)
        wait_all(*ex_b, True)

        z = prec_s[...] * r_s[...]
        d = z + beta * d_s[...]
        d_s[...] = d
        dd = damp_s[...] * d * d
        u_d[...] = u_z[...] + beta.reshape(1, 1, 128) * u_d[...]

        wait_all(*ex_c, False)

        def put_w(comp, t, value):
            w_s[comp, pl.ds(t, 1), :] = u_d[comp, pl.ds(t, 1), :] - value

        gather(3, lambda k, half: buf_c[:, 4 * half + k, :], pidx, ohp, jpf, put_w)

        dot_part = dd[0:8] + dd[8:16] + dd[16:24]
        w0, w1 = w_s[0], w_s[1]
        prod = u_d[0] * w0 + u_d[1] * w1
        for g in range(tiles // 8):
            dot_part = dot_part + prod[8 * g : 8 * g + 8]
        buf_s[ci] = dot_part
        send_all(*ex_s)
        wait_all(*ex_c, True)

        for k in range(9):
            put_term(k, jcf[k] * w0 + jcf[9 + k] * w1)
        scatter(9, cidx, ohc)
        wait_all(*ex_s, False)
        dots = buf_s[0]
        for share in range(1, n_cam):
            dots = dots + buf_s[share]
        dots = jnp.sum(dots, axis=0, keepdims=True)
        for share in range(n_pt):
            msg_d[share, 0:9, :] = part_sum(9, share, 0)
            msg_d[share, 9:18, :] = part_sum(9, share, 1)
            msg_d[share, 18:19, :] = dots
            msg_d[share, 19:24, :] = jnp.zeros((5, 128), f32)
        buf_d[pi] = msg_d[pi]
        send_all(*ex_d)
        wait_all(*ex_s, True)
        wait_all(*ex_d, False)
        img = buf_d[0]
        for share in range(1, n_pt):
            img = img + buf_d[share]
        step_len = energy / jnp.broadcast_to(jnp.sum(img[18:19, :], axis=1, keepdims=True), (1, 128))
        img = jnp.where(lax.broadcasted_iota(i32, (24, 128), 0) < 18, img, 0.0) + damp_s[...] * d
        x_s[...] = x_s[...] + step_len * d
        r_s[...] = r_s[...] - step_len * img

        @pl.when(it < ITERS - 1)
        def _():
            start_a()
            send_all(*ex_a)

        wait_all(*ex_d, True)
        return carry

    lax.fori_loop(0, ITERS, iteration, 0)

    x_out[:, 0:128] = x_s[0:9, :]
    x_out[:, 128:256] = x_s[9:18, :]
    r_out[:, 0:128] = r_s[0:9, :]
    r_out[:, 128:256] = r_s[9:18, :]


def on_device(
    right_side, precond_diag, camera_damping, point_damping,
    camera_jacobian, point_jacobian, camera_index, point_index, tile_count,
):
    n_cam, n_pt = lax.axis_size("cam"), lax.axis_size("pt")
    tiles = camera_index.shape[2]
    obs = tiles * 128
    vm = pl.BlockSpec(memory_space=pltpu.VMEM)
    share = jax.ShapeDtypeStruct(right_side.shape, f32)
    vmem = pltpu.VMEM
    dma = pltpu.SemaphoreType.DMA
    return pl.pallas_call(
        functools.partial(kernel, n_cam, n_pt, tiles),
        out_shape=(share, share),
        in_specs=[vm] * 8 + [pl.BlockSpec(memory_space=pltpu.SMEM)],
        out_specs=(vm, vm),
        scratch_shapes=[
            vmem((LO, obs), bf16), vmem((LO, obs), bf16),
            vmem((18, tiles, 128), f32), vmem((6, tiles, 128), f32),
            vmem((9 * HI, LO), bf16), vmem((9 * HI, LO), bf16),
            vmem((2, 9, tiles, 128), f32), vmem((18 * HI, GRP * 128), bf16), vmem((2, 18 * HI, 128), f32),
            vmem((2, tiles, 128), f32), vmem((2, tiles, 128), f32), vmem((2, tiles, 128), f32),
            vmem((24, 128), f32), vmem((24, 128), f32), vmem((24, 128), f32), vmem((24, 128), f32),
            vmem((24, 128), f32), vmem((8, 128), f32), vmem((16, 128), f32), vmem((1, 128), f32),
            vmem((HI, 24, 128), f32),
            vmem((HI, 8, 128), f32), vmem((HI, 8, 128), f32),
            vmem((HI, 8, 128), f32), vmem((HI, 8, 128), f32),
            vmem((HI, 24, 128), f32), vmem((HI, 24, 128), f32),
            vmem((HI, 16, 128), f32), vmem((HI, 16, 128), f32),
            *[dma((HI,)) for _ in range(12)],
        ],
        compiler_params=pltpu.CompilerParams(
            collective_id=0, has_side_effects=True, vmem_limit_bytes=48 << 20
        ),
        name="pcg",
    )(
        right_side, precond_diag, camera_damping, point_damping.reshape(3, -1),
        camera_jacobian.reshape(18, tiles, 128), point_jacobian.reshape(6, tiles, 128),
        camera_index.reshape(tiles, 128), point_index.reshape(tiles, 128), tile_count,
    )


def solution(mesh):
    return jax.shard_map(
        on_device,
        mesh=mesh,
        in_specs=(
            P(None, ("cam", "pt")),
            P(None, ("cam", "pt")),
            P(None, ("cam", "pt")),
            P(None, "cam", "pt"),
            P("cam", "pt", None, None, None),
            P("cam", "pt", None, None, None),
            P("cam", "pt", None, None),
            P("cam", "pt", None, None),
            P("cam", "pt"),
        ),
        out_specs=(P(None, ("cam", "pt")), P(None, ("cam", "pt"))),
        check_vma=False,
    )
```

```python
import functools

import jax
import jax.numpy as jnp
from jax import lax
from jax.experimental import pallas as pl
from jax.experimental.pallas import tpu as pltpu
from jax.sharding import PartitionSpec as P

ITERS = 3
MESH = pl.DeviceIdType.MESH
f32, bf16, i32 = jnp.float32, jnp.bfloat16, jnp.int32

PAIRS = ((0, 0), (0, 1), (0, 2), (1, 1), (1, 2), (2, 2))
SYM = ((0, 1, 2), (1, 3, 4), (2, 4, 5))
CHUNK = 16
LANES = lax.GatherDimensionNumbers(
    offset_dims=(), collapsed_slice_dims=(1,), start_index_map=(1,),
    operand_batching_dims=(0,), start_indices_batching_dims=(0,),
)


def lane_gather(rows, lanes):
    return lax.gather(rows, lanes[..., None], LANES, (1, 1), mode=lax.GatherScatterMode.PROMISE_IN_BOUNDS)


def ring(off, size):
    return min(off, size - off)


def offsets(major, minor, near_minor):
    return sorted(
        (ring(a, major) + (0.1 if near_minor else 1) * ring(b, minor), a, b)
        for a in range(major) for b in range(minor) if a or b
    )


def split_by(offs, edges):
    groups, low = [], -1
    for edge in edges:
        part = [off for off in offs if low < off[0] <= edge]
        if part:
            groups.append(part)
        low = edge
    return groups


def kernel(
    n_cam, n_pt, tiles,
    rhs_h, pre_h, damp_h, pdamp_h, jc_h, jp_h, cidx_h, pidx_h, tcount_h,
    x_out, r_out,
    rhs, pre, damp, pdamp, jc, jp, cidx, pidx, tcount, isem,
    ohc, ohp, jcf, jpf, term, amat, acc, vals,
    u_z, u_d,
    prec_s, damp_s, x_s, r_s, d_s, pz_s, inv_s, gam_s,
    buf_a, msg_b, buf_b, buf_c, buf_s, msg_d, buf_d, msg_h, buf_h,
    sa, ra, sb, rb, sc, rc, ss, rs, sd, rd, sh, rh,
):
    ci = lax.axis_index("cam")
    pi = lax.axis_index("pt")
    groups = tiles // 8
    pt_dims = (n_pt // 4, 4) if n_pt >= 4 else (1, n_pt)
    cam_dims = (n_cam // 2, 2)
    pt_offs = offsets(*pt_dims, False)
    cam_offs = offsets(*cam_dims, True)

    def peer_at(me, dims, off):
        major = lax.rem(lax.div(me, dims[1]) + off[1], dims[0])
        minor = lax.rem(lax.rem(me, dims[1]) + off[2], dims[1])
        return major * dims[1] + minor

    def cam_peer(off):
        return peer_at(ci, cam_dims, off)

    def pt_peer(off):
        return peer_at(pi, pt_dims, off)

    def cam_id(peer):
        return (peer, pi)

    def pt_id(peer):
        return (ci, peer)

    on_cam = (cam_offs, cam_peer, cam_id, ci)
    on_pt = (pt_offs, pt_peer, pt_id, pi)

    def ship(group, peer, src, dst, send_sem, recv_sem):
        me = group[3]
        return pltpu.make_async_remote_copy(
            src_ref=src, dst_ref=dst.at[me],
            send_sem=send_sem.at[peer], recv_sem=recv_sem.at[me],
            device_id=group[2](peer), device_id_type=MESH,
        )

    def send_all(group, src_of, dst, send_sem, recv_sem, fill=None):
        for off in reversed(group[0]):
            peer = group[1](off)
            if fill is not None:
                fill(peer)
            ship(group, peer, src_of(peer), dst, send_sem, recv_sem).start()

    def wait_sent(group, src_of, dst, send_sem, recv_sem):
        for off in group[0]:
            peer = group[1](off)
            ship(group, peer, src_of(peer), dst, send_sem, recv_sem).wait_send()

    def wait_some(group, part, dst, recv_sem):
        for off in part:
            peer = group[1](off)
            pltpu.make_async_remote_copy(
                src_ref=dst.at[peer], dst_ref=dst.at[peer],
                send_sem=recv_sem.at[peer], recv_sem=recv_sem.at[peer],
                device_id=group[2](peer), device_id_type=MESH,
            ).wait_recv()

    ex_a = (on_pt, lambda peer: buf_a.at[pi], buf_a, sa, ra)
    ex_b = (on_cam, lambda peer: msg_b.at[peer], buf_b, sb, rb)
    ex_c = (on_cam, lambda peer: buf_c.at[ci], buf_c, sc, rc)
    ex_s = (on_cam, lambda peer: buf_s.at[ci], buf_s, ss, rs)
    ex_d = (on_pt, lambda peer: msg_d.at[peer], buf_d, sd, rd)
    ex_h = (on_cam, lambda peer: msg_h.at[peer], buf_h, sh, rh)

    barrier = pltpu.get_barrier_semaphore()

    def greet(group):
        for off in reversed(group[0]):
            pl.semaphore_signal(barrier, inc=1, device_id=group[2](group[1](off)), device_id_type=MESH)

    greet(on_pt)
    greet(on_cam)

    loads = [
        pltpu.make_async_copy(src, dst, isem.at[n])
        for n, (src, dst) in enumerate(
            ((rhs_h, rhs), (pre_h, pre), (tcount_h, tcount), (jp_h, jp), (pidx_h, pidx),
             (jc_h, jc), (cidx_h, cidx), (damp_h, damp), (pdamp_h, pdamp))
        )
    ]
    for load in loads:
        load.start()

    def to_share(src, dst):
        dst[...] = jnp.zeros((24, 128), f32)
        dst[0:9, :] = src[:, 0:128]
        dst[9:18, :] = src[:, 128:256]

    x_s[...] = jnp.zeros((24, 128), f32)
    d_s[...] = jnp.zeros((24, 128), f32)
    pz_s[...] = jnp.zeros((8, 128), f32)
    u_d[...] = jnp.zeros_like(u_d)
    gam_s[...] = jnp.ones((1, 128), f32)

    def put_a():
        r = r_s[...]
        z = prec_s[...] * r
        buf_a[pi] = z
        buf_a[pi, 18:19, :] = jnp.sum(r * z, axis=0, keepdims=True)

    loads[0].wait()
    loads[1].wait()
    to_share(rhs, r_s)
    to_share(pre, prec_s)
    put_a()

    for load in loads[2:]:
        load.wait()
    to_share(damp, damp_s)
    live = lax.broadcasted_iota(i32, (tiles, 128), 0) < tcount[0, 0]
    for row in range(6):
        jpf[row] = jnp.where(live, jp[row].astype(f32), 0.0)
    for row in range(18):
        jcf[row] = jnp.where(live, jc[row].astype(f32), 0.0)

    def one_hot(idx, low, dst):
        iota = lax.broadcasted_iota(i32, (low, 128), 0)

        def one(t, carry):
            part = jnp.broadcast_to(idx[pl.ds(t, 1), :] & (low - 1), (low, 128))
            dst[:, pl.ds(pl.multiple_of(t * 128, 128), 128)] = jnp.where(part == iota, 1.0, 0.0).astype(bf16)
            return carry

        lax.fori_loop(0, tiles, one, 0, unroll=4)

    one_hot(pidx, 128, ohp)
    pl.semaphore_wait(barrier, (n_pt - 1) + (n_cam - 1))
    send_all(*ex_a)

    def put_term(k, at, value):
        high = value.astype(bf16).astype(f32)
        term[0, k, at, :] = high
        term[1, k, at, :] = value - high

    def scatter(nk, idx, oh, low):
        shift, high = (8, 16) if low == 256 else (7, 32)
        iota = lax.broadcasted_iota(i32, (high, 128), 0)
        rows = 2 * nk * high

        def build(c):
            for t in range(c * CHUNK, min(c * CHUNK + CHUNK, tiles)):
                m = jnp.broadcast_to(idx[t : t + 1, :] >> shift, (high, 128)) == iota
                for part in range(2):
                    for k in range(nk):
                        row = jnp.broadcast_to(term[part, k, t : t + 1, :], (high, 128))
                        at = (part * nk + k) * high
                        amat[at : at + high, t * 128 : t * 128 + 128] = jnp.where(m, row, 0.0).astype(bf16)

        chunks = pl.cdiv(tiles, CHUNK)
        build(0)
        for c in range(chunks):
            if c + 1 < chunks:
                build(c + 1)
            cols = slice(c * CHUNK * 128, min(c * CHUNK + CHUNK, tiles) * 128)
            res = lax.dot_general(
                amat[0:rows, cols], oh[:, cols], (((1,), (1,)), ((), ())), preferred_element_type=f32
            )
            for half in range(low // 128):
                mine = res[:, half * 128 : half * 128 + 128]
                if c:
                    mine = mine + acc[half, 0:rows, :]
                acc[half, 0:rows, :] = mine

    def point_rows(nk, share, half):
        at = 2 * share + half
        return acc[0, pl.ds(at, nk, stride=32), :] + acc[0, pl.ds(at + 32 * nk, nk, stride=32), :]

    def camera_rows(share, half):
        return acc[half, pl.ds(share, 9, stride=16), :] + acc[half, pl.ds(share + 144, 9, stride=16), :]

    def gather(nk, group, parts, table, row_of, recv_sem, idx, done):
        for n, part in enumerate(parts):
            wait_some(group, part, table, recv_sem)
            peers = [group[1](off) for off in part]
            if n == 0:
                peers = [group[3], *peers]
            last = n == len(parts) - 1

            def one(g, carry):
                at = pl.ds(pl.multiple_of(g * 8, 8), 8)
                own = idx[at, :]
                lanes, high = own & 127, own >> 7
                got = [vals[k, at, :] if n else jnp.zeros((8, 128), f32) for k in range(nk)]
                for peer in peers:
                    for half in range(2):
                        m = high == 2 * peer + half
                        for k in range(nk):
                            row = jnp.broadcast_to(table[peer, pl.ds(row_of(k, half), 1), :], (8, 128))
                            got[k] = jnp.where(m, lane_gather(row, lanes), got[k])
                if last:
                    done(at, got)
                else:
                    for k in range(nk):
                        vals[k, at, :] = got[k]
                return carry

            lax.fori_loop(0, groups, one, 0, unroll=max(1, min(groups, 144 // (2 * nk * len(peers)))))

    for k, (a, b) in enumerate(PAIRS):
        put_term(k, slice(None), jpf[a] * jpf[b] + jpf[3 + a] * jpf[3 + b])
    scatter(6, pidx, ohp, 128)

    def fill_h(share):
        msg_h[share, 0:6, :] = point_rows(6, share, 0)
        msg_h[share, 8:14, :] = point_rows(6, share, 1)
        msg_h[share, 6:8, :] = jnp.zeros((2, 128), f32)
        msg_h[share, 14:16, :] = jnp.zeros((2, 128), f32)

    send_all(*ex_h, fill_h)
    fill_h(ci)
    buf_h[ci] = msg_h[ci]

    def solve_curvature():
        wait_some(on_cam, cam_offs, buf_h, rh)
        h = buf_h[0]
        for share in range(1, n_cam):
            h = h + buf_h[share]
        for half in range(2):
            lanes = slice(half * 128, half * 128 + 128)
            e = [h[8 * half + k : 8 * half + k + 1, :] for k in range(6)]
            e[0] = e[0] + pdamp[0, :, lanes]
            e[3] = e[3] + pdamp[1, :, lanes]
            e[5] = e[5] + pdamp[2, :, lanes]
            a1 = e[3] * e[5] - e[4] * e[4]
            a2 = e[2] * e[4] - e[1] * e[5]
            a3 = e[1] * e[4] - e[2] * e[3]
            a4 = e[0] * e[5] - e[2] * e[2]
            a5 = e[1] * e[2] - e[0] * e[4]
            a6 = e[0] * e[3] - e[1] * e[1]
            det = e[0] * a1 + e[1] * a2 + e[2] * a3
            for k, value in enumerate((a1, a2, a3, a4, a5, a6)):
                inv_s[8 * half + k : 8 * half + k + 1, :] = value / det
        wait_sent(*ex_h)

    def iteration(it, carry):
        def put_u(at, v):
            u0 = sum(jcf[k, at, :] * v[k] for k in range(9))
            u1 = sum(jcf[9 + k, at, :] * v[k] for k in range(9))
            u_z[0, at, :] = u0
            u_z[1, at, :] = u1
            for k in range(3):
                put_term(k, at, jpf[k, at, :] * u0 + jpf[3 + k, at, :] * u1)

        gather(9, on_pt, split_by(pt_offs, (1, 2, 3, 9)), buf_a, lambda k, half: 9 * half + k, ra, cidx, put_u)
        grow = buf_a[0, 18:19, :]
        for share in range(1, n_pt):
            grow = grow + buf_a[share, 18:19, :]

        scatter(3, pidx, ohp, 128)

        def fill_b(share):
            msg_b[share, 0:3, :] = point_rows(3, share, 0)
            msg_b[share, 4:7, :] = point_rows(3, share, 1)
            msg_b[share, 3:4, :] = grow
            msg_b[share, 7:8, :] = jnp.zeros((1, 128), f32)

        send_all(*ex_b, fill_b)
        fill_b(ci)
        buf_b[ci] = msg_b[ci]
        wait_sent(*ex_a)

        @pl.when(it == 0)
        def _():
            one_hot(cidx, 256, ohc)
            solve_curvature()

        wait_some(on_cam, cam_offs, buf_b, rb)
        pz = buf_b[0]
        for share in range(1, n_cam):
            pz = pz + buf_b[share]
        energy = jnp.broadcast_to(jnp.sum(pz[3:4, :], axis=1, keepdims=True), (1, 128))
        beta = jnp.where(it == 0, 0.0, energy / gam_s[...])
        gam_s[...] = energy
        pd = pz + beta * pz_s[...]
        pz_s[...] = pd
        for half in range(2):
            v = [pd[4 * half + k : 4 * half + k + 1, :] for k in range(3)]
            m = [inv_s[8 * half + k : 8 * half + k + 1, :] for k in range(6)]
            for row in range(3):
                at = 4 * half + row
                buf_c[ci, at : at + 1, :] = sum(m[SYM[row][col]] * v[col] for col in range(3))
            buf_c[ci, 4 * half + 3 : 4 * half + 4, :] = jnp.zeros((1, 128), f32)
        send_all(*ex_c)

        d = prec_s[...] * r_s[...] + beta * d_s[...]
        d_s[...] = d
        dd = damp_s[...] * d * d
        u_d[...] = u_z[...] + beta.reshape(1, 1, 128) * u_d[...]
        buf_s[ci] = dd[0:8] + dd[8:16] + dd[16:24]
        wait_sent(*ex_b)

        def put_w(at, q):
            u0, u1 = u_d[0, at, :], u_d[1, at, :]
            w0 = u0 - sum(jpf[k, at, :] * q[k] for k in range(3))
            w1 = u1 - sum(jpf[3 + k, at, :] * q[k] for k in range(3))
            buf_s[ci] = buf_s[ci] + (u0 * w0 + u1 * w1)
            for k in range(9):
                put_term(k, at, jcf[k, at, :] * w0 + jcf[9 + k, at, :] * w1)

        gather(
            3, on_cam, split_by(cam_offs, (1.5, 2.5, 3.5, 9)), buf_c, lambda k, half: 4 * half + k, rc, pidx, put_w
        )
        send_all(*ex_s)

        scatter(9, cidx, ohc, 256)
        wait_some(on_cam, cam_offs, buf_s, rs)
        dots = buf_s[0]
        for share in range(1, n_cam):
            dots = dots + buf_s[share]
        dots = jnp.sum(dots, axis=0, keepdims=True)

        def fill_d(share):
            msg_d[share, 0:9, :] = camera_rows(share, 0)
            msg_d[share, 9:18, :] = camera_rows(share, 1)
            msg_d[share, 18:19, :] = dots
            msg_d[share, 19:24, :] = jnp.zeros((5, 128), f32)

        send_all(*ex_d, fill_d)
        fill_d(pi)
        buf_d[pi] = msg_d[pi]
        wait_sent(*ex_c)
        wait_sent(*ex_s)
        wait_some(on_pt, pt_offs, buf_d, rd)
        img = buf_d[0]
        for share in range(1, n_pt):
            img = img + buf_d[share]
        step_len = energy / jnp.broadcast_to(jnp.sum(img[18:19, :], axis=1, keepdims=True), (1, 128))
        img = jnp.where(lax.broadcasted_iota(i32, (24, 128), 0) < 18, img, 0.0) + damp_s[...] * d
        x_s[...] = x_s[...] + step_len * d
        r_s[...] = r_s[...] - step_len * img

        @pl.when(it < ITERS - 1)
        def _():
            put_a()
            send_all(*ex_a)

        wait_sent(*ex_d)
        return carry

    lax.fori_loop(0, ITERS, iteration, 0)

    x_out[:, 0:128] = x_s[0:9, :]
    x_out[:, 128:256] = x_s[9:18, :]
    r_out[:, 0:128] = r_s[0:9, :]
    r_out[:, 128:256] = r_s[9:18, :]


def on_device(
    right_side, precond_diag, camera_damping, point_damping,
    camera_jacobian, point_jacobian, camera_index, point_index, tile_count,
):
    n_cam, n_pt = lax.axis_size("cam"), lax.axis_size("pt")
    tiles = camera_index.shape[2]
    obs = tiles * 128
    vm = pl.BlockSpec(memory_space=pltpu.VMEM)
    share = jax.ShapeDtypeStruct(right_side.shape, f32)
    vmem = pltpu.VMEM
    dma = pltpu.SemaphoreType.DMA
    slots = 16
    return pl.pallas_call(
        functools.partial(kernel, n_cam, n_pt, tiles),
        out_shape=(share, share),
        in_specs=[pl.BlockSpec(memory_space=pl.ANY)] * 9,
        out_specs=(vm, vm),
        scratch_shapes=[
            vmem(right_side.shape, f32), vmem(right_side.shape, f32), vmem(right_side.shape, f32),
            vmem(point_damping.shape, f32),
            vmem((18, tiles, 128), bf16), vmem((6, tiles, 128), bf16),
            vmem((tiles, 128), i32), vmem((tiles, 128), i32), pltpu.SMEM((1, 1), i32), dma((9,)),
            vmem((256, obs), bf16), vmem((128, obs), bf16),
            vmem((18, tiles, 128), f32), vmem((6, tiles, 128), f32),
            vmem((2, 9, tiles, 128), f32), vmem((384, obs), bf16), vmem((2, 384, 128), f32),
            vmem((9, tiles, 128), f32),
            vmem((2, tiles, 128), f32), vmem((2, tiles, 128), f32),
            vmem((24, 128), f32), vmem((24, 128), f32), vmem((24, 128), f32), vmem((24, 128), f32),
            vmem((24, 128), f32), vmem((8, 128), f32), vmem((16, 128), f32), vmem((1, 128), f32),
            vmem((slots, 24, 128), f32),
            vmem((slots, 8, 128), f32), vmem((slots, 8, 128), f32),
            vmem((slots, 8, 128), f32), vmem((slots, 8, 128), f32),
            vmem((slots, 24, 128), f32), vmem((slots, 24, 128), f32),
            vmem((slots, 16, 128), f32), vmem((slots, 16, 128), f32),
            *[dma((slots,)) for _ in range(12)],
        ],
        compiler_params=pltpu.CompilerParams(
            collective_id=0, has_side_effects=True, vmem_limit_bytes=60 << 20
        ),
        name="pcg",
    )(
        right_side, precond_diag, camera_damping, point_damping,
        camera_jacobian.reshape(18, tiles, 128), point_jacobian.reshape(6, tiles, 128),
        camera_index.reshape(tiles, 128), point_index.reshape(tiles, 128), tile_count,
    )


def solution(mesh):
    return jax.shard_map(
        on_device,
        mesh=mesh,
        in_specs=(
            P(None, ("cam", "pt")),
            P(None, ("cam", "pt")),
            P(None, ("cam", "pt")),
            P(None, "cam", "pt"),
            P("cam", "pt", None, None, None),
            P("cam", "pt", None, None, None),
            P("cam", "pt", None, None),
            P("cam", "pt", None, None),
            P("cam", "pt"),
        ),
        out_specs=(P(None, ("cam", "pt")), P(None, ("cam", "pt"))),
        check_vma=False,
    )
```

```python
import functools

import jax
import jax.numpy as jnp
from jax import lax
from jax.experimental import pallas as pl
from jax.experimental.pallas import tpu as pltpu
from jax.sharding import PartitionSpec as P

ITERS = 3
MESH = pl.DeviceIdType.MESH
f32, bf16, i32 = jnp.float32, jnp.bfloat16, jnp.int32

PAIRS = ((0, 0), (0, 1), (0, 2), (1, 1), (1, 2), (2, 2))
SYM = ((0, 1, 2), (1, 3, 4), (2, 4, 5))
CHUNK = 16
LANES = lax.GatherDimensionNumbers(
    offset_dims=(), collapsed_slice_dims=(1,), start_index_map=(1,),
    operand_batching_dims=(0,), start_indices_batching_dims=(0,),
)


def lane_gather(rows, lanes):
    return lax.gather(rows, lanes[..., None], LANES, (1, 1), mode=lax.GatherScatterMode.PROMISE_IN_BOUNDS)


def ring(off, size):
    return min(off, size - off)


def offsets(major, minor, near_minor):
    return sorted(
        (ring(a, major) + (0.1 if near_minor else 1) * ring(b, minor), a, b)
        for a in range(major) for b in range(minor) if a or b
    )


def split_by(offs, edges):
    groups, low = [], -1
    for edge in edges:
        part = [off for off in offs if low < off[0] <= edge]
        if part:
            groups.append(part)
        low = edge
    return groups


def kernel(
    n_cam, n_pt, tiles,
    rhs_h, pre_h, damp_h, pdamp_h, jc_h, jp_h, cidx_h, pidx_h, tcount_h,
    x_out, r_out, d_out, img_out, step_out,
    rhs, pre, damp, pdamp, jc, jp, cidx, pidx, tcount, isem,
    ohc, ohp, jcf, jpf, term, amat, acc, vals,
    u_z, u_d,
    prec_s, damp_s, x_s, r_s, d_s, img_s, pz_s, inv_s, gam_s,
    buf_a, msg_b, buf_b, buf_c, msg_d, buf_d, msg_h, buf_h,
    sa, ra, sb, rb, sc, rc, sd, rd, sh, rh,
):
    ci = lax.axis_index("cam")
    pi = lax.axis_index("pt")
    groups = tiles // 8
    pt_dims = (n_pt // 4, 4) if n_pt >= 4 else (1, n_pt)
    cam_dims = (n_cam // 2, 2)
    pt_offs = offsets(*pt_dims, False)
    cam_offs = offsets(*cam_dims, True)

    def peer_at(me, dims, off):
        major = lax.rem(lax.div(me, dims[1]) + off[1], dims[0])
        minor = lax.rem(lax.rem(me, dims[1]) + off[2], dims[1])
        return major * dims[1] + minor

    def cam_peer(off):
        return peer_at(ci, cam_dims, off)

    def pt_peer(off):
        return peer_at(pi, pt_dims, off)

    def cam_id(peer):
        return (peer, pi)

    def pt_id(peer):
        return (ci, peer)

    on_cam = (cam_offs, cam_peer, cam_id, ci)
    on_pt = (pt_offs, pt_peer, pt_id, pi)

    def ship(group, peer, src, dst, send_sem, recv_sem):
        me = group[3]
        return pltpu.make_async_remote_copy(
            src_ref=src, dst_ref=dst.at[me],
            send_sem=send_sem.at[peer], recv_sem=recv_sem.at[me],
            device_id=group[2](peer), device_id_type=MESH,
        )

    def send_all(group, src_of, dst, send_sem, recv_sem, fill=None):
        for off in reversed(group[0]):
            peer = group[1](off)
            if fill is not None:
                fill(peer)
            ship(group, peer, src_of(peer), dst, send_sem, recv_sem).start()

    def wait_sent(group, src_of, dst, send_sem, recv_sem):
        for off in group[0]:
            peer = group[1](off)
            ship(group, peer, src_of(peer), dst, send_sem, recv_sem).wait_send()

    def wait_some(group, part, dst, recv_sem):
        for off in part:
            peer = group[1](off)
            pltpu.make_async_remote_copy(
                src_ref=dst.at[peer], dst_ref=dst.at[peer],
                send_sem=recv_sem.at[peer], recv_sem=recv_sem.at[peer],
                device_id=group[2](peer), device_id_type=MESH,
            ).wait_recv()

    ex_a = (on_pt, lambda peer: buf_a.at[pi], buf_a, sa, ra)
    ex_b = (on_cam, lambda peer: msg_b.at[peer], buf_b, sb, rb)
    ex_c = (on_cam, lambda peer: buf_c.at[ci], buf_c, sc, rc)
    ex_d = (on_pt, lambda peer: msg_d.at[peer], buf_d, sd, rd)
    ex_h = (on_cam, lambda peer: msg_h.at[peer], buf_h, sh, rh)

    barrier = pltpu.get_barrier_semaphore()

    def greet(group):
        for off in reversed(group[0]):
            pl.semaphore_signal(barrier, inc=1, device_id=group[2](group[1](off)), device_id_type=MESH)

    loads = [
        pltpu.make_async_copy(src, dst, isem.at[n])
        for n, (src, dst) in enumerate(
            ((rhs_h, rhs), (pre_h, pre), (tcount_h, tcount), (jp_h, jp), (pidx_h, pidx),
             (jc_h, jc), (cidx_h, cidx), (damp_h, damp), (pdamp_h, pdamp))
        )
    ]
    for load in loads:
        load.start()

    greet(on_pt)
    greet(on_cam)

    def to_share(src, dst):
        dst[...] = jnp.zeros((24, 128), f32)
        dst[0:9, :] = src[:, 0:128]
        dst[9:18, :] = src[:, 128:256]

    def from_share(value, dst):
        dst[:, 0:128] = value[0:9]
        dst[:, 128:256] = value[9:18]

    x_s[...] = jnp.zeros((24, 128), f32)
    img_s[...] = jnp.zeros((24, 128), f32)
    d_s[...] = jnp.zeros((24, 128), f32)
    pz_s[...] = jnp.zeros((7, 128), f32)
    u_d[...] = jnp.zeros_like(u_d)
    gam_s[...] = jnp.ones((1, 128), f32)

    def put_a():
        r = r_s[...]
        z = prec_s[...] * r
        buf_a[pi, 0:18, :] = z[0:18]
        buf_a[pi, 18:19, :] = jnp.sum(r * z, axis=0, keepdims=True)

    loads[0].wait()
    loads[1].wait()
    to_share(rhs, r_s)
    to_share(pre, prec_s)
    put_a()

    for load in loads[2:]:
        load.wait()
    to_share(damp, damp_s)
    live = lax.broadcasted_iota(i32, (tiles, 128), 0) < tcount[0, 0]
    for row in range(6):
        jpf[row] = jnp.where(live, jp[row].astype(f32), 0.0)
    for row in range(18):
        jcf[row] = jnp.where(live, jc[row].astype(f32), 0.0)

    def one_hot(idx, low, dst):
        iota = lax.broadcasted_iota(i32, (low, 128), 0)

        def one(t, carry):
            part = jnp.broadcast_to(idx[pl.ds(t, 1), :] & (low - 1), (low, 128))
            dst[:, pl.ds(pl.multiple_of(t * 128, 128), 128)] = jnp.where(part == iota, 1.0, 0.0).astype(bf16)
            return carry

        lax.fori_loop(0, tiles, one, 0, unroll=4)

    one_hot(pidx, 128, ohp)

    def put_term(k, at, value):
        high = value.astype(bf16).astype(f32)
        term[0, k, at, :] = high
        term[1, k, at, :] = value - high

    def scatter(nk, idx, oh, low):
        shift, high = (8, 16) if low == 256 else (7, 32)
        iota = lax.broadcasted_iota(i32, (high, 128), 0)
        rows = 2 * nk * high

        def build(c):
            for t in range(c * CHUNK, min(c * CHUNK + CHUNK, tiles)):
                m = jnp.broadcast_to(idx[t : t + 1, :] >> shift, (high, 128)) == iota
                for part in range(2):
                    for k in range(nk):
                        row = jnp.broadcast_to(term[part, k, t : t + 1, :], (high, 128))
                        at = (part * nk + k) * high
                        amat[at : at + high, t * 128 : t * 128 + 128] = jnp.where(m, row, 0.0).astype(bf16)

        chunks = pl.cdiv(tiles, CHUNK)
        build(0)
        for c in range(chunks):
            if c + 1 < chunks:
                build(c + 1)
            cols = slice(c * CHUNK * 128, min(c * CHUNK + CHUNK, tiles) * 128)
            res = lax.dot_general(
                amat[0:rows, cols], oh[:, cols], (((1,), (1,)), ((), ())), preferred_element_type=f32
            )
            for half in range(low // 128):
                mine = res[:, half * 128 : half * 128 + 128]
                if c:
                    mine = mine + acc[half, 0:rows, :]
                acc[half, 0:rows, :] = mine

    def point_rows(nk, share, half):
        at = 2 * share + half
        return acc[0, pl.ds(at, nk, stride=32), :] + acc[0, pl.ds(at + 32 * nk, nk, stride=32), :]

    def camera_rows(share, half):
        return acc[half, pl.ds(share, 9, stride=16), :] + acc[half, pl.ds(share + 144, 9, stride=16), :]

    def unroll_of(count):
        return 8 if count <= 24 else 4 if count <= 60 else 2

    def gather(nk, group, parts, table, row_of, recv_sem, idx, done):
        for n, part in enumerate(parts):
            wait_some(group, part, table, recv_sem)
            peers = [group[1](off) for off in part] if part else [group[3]]
            last = n == len(parts) - 1

            def one(g, carry):
                at = pl.ds(pl.multiple_of(g * 8, 8), 8)
                own = idx[at, :]
                lanes, high = own & 127, own >> 7
                got = [vals[k, at, :] if n else jnp.zeros((8, 128), f32) for k in range(nk)]
                for peer in peers:
                    for half in range(2):
                        m = high == 2 * peer + half
                        for k in range(nk):
                            row = jnp.broadcast_to(table[peer, pl.ds(row_of(k, half), 1), :], (8, 128))
                            got[k] = jnp.where(m, lane_gather(row, lanes), got[k])
                if last:
                    done(at, got)
                else:
                    for k in range(nk):
                        vals[k, at, :] = got[k]
                return carry

            lax.fori_loop(0, groups, one, 0, unroll=min(groups, unroll_of(2 * nk * len(peers))))

    for k, (a, b) in enumerate(PAIRS):
        put_term(k, slice(None), jpf[a] * jpf[b] + jpf[3 + a] * jpf[3 + b])
    acc[0] = jnp.zeros((384, 128), f32)
    iota_h = lax.broadcasted_iota(i32, (32, 128), 0)
    chunk_h = min(CHUNK, tiles)

    def curvature(c, carry):
        @pl.when(c == 1)
        def _():
            pl.semaphore_wait(barrier, (n_pt - 1) + (n_cam - 1))
            send_all(*ex_a)

        for s in range(chunk_h):
            t = c * chunk_h + s
            m = jnp.broadcast_to(pidx[pl.ds(t, 1), :] >> 7, (32, 128)) == iota_h
            for part in range(2):
                for k in range(6):
                    row = jnp.broadcast_to(term[part, k, pl.ds(t, 1), :], (32, 128))
                    at = (part * 6 + k) * 32
                    amat[at : at + 32, s * 128 : s * 128 + 128] = jnp.where(m, row, 0.0).astype(bf16)
        size = chunk_h * 128
        acc[0] += lax.dot_general(
            amat[:, 0:size], ohp[:, pl.ds(pl.multiple_of(c * size, 128), size)],
            (((1,), (1,)), ((), ())), preferred_element_type=f32,
        )
        return carry

    lax.fori_loop(0, tiles // chunk_h, curvature, 0)

    def fill_h(share):
        msg_h[share, 0:6, :] = point_rows(6, share, 0)
        msg_h[share, 8:14, :] = point_rows(6, share, 1)
        msg_h[share, 6:8, :] = jnp.zeros((2, 128), f32)
        msg_h[share, 14:16, :] = jnp.zeros((2, 128), f32)

    send_all(*ex_h, fill_h)
    fill_h(ci)
    buf_h[ci] = msg_h[ci]

    def solve_curvature():
        wait_some(on_cam, cam_offs, buf_h, rh)
        h = buf_h[0]
        for share in range(1, n_cam):
            h = h + buf_h[share]
        for half in range(2):
            lanes = slice(half * 128, half * 128 + 128)
            e = [h[8 * half + k : 8 * half + k + 1, :] for k in range(6)]
            e[0] = e[0] + pdamp[0, :, lanes]
            e[3] = e[3] + pdamp[1, :, lanes]
            e[5] = e[5] + pdamp[2, :, lanes]
            a1 = e[3] * e[5] - e[4] * e[4]
            a2 = e[2] * e[4] - e[1] * e[5]
            a3 = e[1] * e[4] - e[2] * e[3]
            a4 = e[0] * e[5] - e[2] * e[2]
            a5 = e[1] * e[2] - e[0] * e[4]
            a6 = e[0] * e[3] - e[1] * e[1]
            det = e[0] * a1 + e[1] * a2 + e[2] * a3
            for k, value in enumerate((a1, a2, a3, a4, a5, a6)):
                inv_s[8 * half + k : 8 * half + k + 1, :] = value / det
        wait_sent(*ex_h)

    def iteration(it, carry):
        def put_u(at, v):
            u0 = sum(jcf[k, at, :] * v[k] for k in range(9))
            u1 = sum(jcf[9 + k, at, :] * v[k] for k in range(9))
            u_z[0, at, :] = u0
            u_z[1, at, :] = u1
            for k in range(3):
                put_term(k, at, jpf[k, at, :] * u0 + jpf[3 + k, at, :] * u1)

        gather(9, on_pt, [[], *split_by(pt_offs, (1, 2, 3, 9))], buf_a, lambda k, half: 9 * half + k, ra, cidx, put_u)
        grow = buf_a[0, 18:19, :]
        for share in range(1, n_pt):
            grow = grow + buf_a[share, 18:19, :]

        scatter(3, pidx, ohp, 128)

        def fill_b(share):
            msg_b[share, 0:3, :] = point_rows(3, share, 0)
            msg_b[share, 4:7, :] = point_rows(3, share, 1)
            msg_b[share, 3:4, :] = grow

        send_all(*ex_b, fill_b)
        fill_b(ci)
        buf_b[ci] = msg_b[ci]
        wait_sent(*ex_a)

        @pl.when(it == 0)
        def _():
            one_hot(cidx, 256, ohc)
            solve_curvature()

        wait_some(on_cam, cam_offs, buf_b, rb)
        pz = buf_b[0]
        for share in range(1, n_cam):
            pz = pz + buf_b[share]
        energy = jnp.broadcast_to(jnp.sum(pz[3:4, :], axis=1, keepdims=True), (1, 128))
        beta = jnp.where(it == 0, 0.0, energy / gam_s[...])
        gam_s[...] = energy
        pd = pz + beta * pz_s[...]
        pz_s[...] = pd
        d = prec_s[...] * r_s[...] + beta * d_s[...]
        d_s[...] = d
        part = jnp.sum(damp_s[...] * d * d, axis=0, keepdims=True)
        squares = jnp.zeros((8, 128), f32)
        for g in range(groups):
            for comp in range(2):
                u = u_z[comp, 8 * g : 8 * g + 8, :] + beta * u_d[comp, 8 * g : 8 * g + 8, :]
                u_d[comp, 8 * g : 8 * g + 8, :] = u
                squares = squares + u * u
        part = part + jnp.sum(squares, axis=0, keepdims=True)
        for half in range(2):
            v = [pd[4 * half + k : 4 * half + k + 1, :] for k in range(3)]
            m = [inv_s[8 * half + k : 8 * half + k + 1, :] for k in range(6)]
            for row in range(3):
                at = 4 * half + row
                q = sum(m[SYM[row][col]] * v[col] for col in range(3))
                buf_c[ci, at : at + 1, :] = q
                part = part - q * v[row]
        buf_c[ci, 3:4, :] = part
        send_all(*ex_c)
        wait_sent(*ex_b)

        def put_w(at, q):
            u0, u1 = u_d[0, at, :], u_d[1, at, :]
            w0 = u0 - sum(jpf[k, at, :] * q[k] for k in range(3))
            w1 = u1 - sum(jpf[3 + k, at, :] * q[k] for k in range(3))
            for k in range(9):
                put_term(k, at, jcf[k, at, :] * w0 + jcf[9 + k, at, :] * w1)

        gather(3, on_cam, [[], *split_by(cam_offs, (0.5, 2.5, 3.5, 9))], buf_c, lambda k, half: 4 * half + k, rc, pidx, put_w)
        dots = buf_c[0, 3:4, :]
        for share in range(1, n_cam):
            dots = dots + buf_c[share, 3:4, :]

        scatter(9, cidx, ohc, 256)

        def fill_d(share):
            msg_d[share, 0:9, :] = camera_rows(share, 0)
            msg_d[share, 9:18, :] = camera_rows(share, 1)
            msg_d[share, 18:19, :] = dots

        send_all(*ex_d, fill_d)
        fill_d(pi)
        buf_d[pi] = msg_d[pi]
        wait_sent(*ex_c)
        wait_some(on_pt, pt_offs, buf_d, rd)
        img = buf_d[0]
        for share in range(1, n_pt):
            img = img + buf_d[share]
        step_len = energy / jnp.broadcast_to(jnp.sum(img[18:19, :], axis=1, keepdims=True), (1, 128))
        img_s[0:18, :] = img[0:18]
        img = img_s[...] + damp_s[...] * d

        @pl.when(it == ITERS - 1)
        def _():
            from_share(img, img_out)
            from_share(d, d_out)
            from_share(x_s[...], x_out)
            from_share(r_s[...], r_out)
            step_out[...] = jnp.broadcast_to(step_len[:, 0:1], step_out.shape)

        @pl.when(it < ITERS - 1)
        def _():
            x_s[...] = x_s[...] + step_len * d
            r_s[...] = r_s[...] - step_len * img
            put_a()
            send_all(*ex_a)

        wait_sent(*ex_d)
        return carry

    lax.fori_loop(0, ITERS, iteration, 0)


def on_device(
    right_side, precond_diag, camera_damping, point_damping,
    camera_jacobian, point_jacobian, camera_index, point_index, tile_count,
):
    n_cam, n_pt = lax.axis_size("cam"), lax.axis_size("pt")
    tiles = camera_index.shape[2]
    obs = tiles * 128
    vm = pl.BlockSpec(memory_space=pltpu.VMEM)
    share = jax.ShapeDtypeStruct(right_side.shape, f32)
    vmem = pltpu.VMEM
    dma = pltpu.SemaphoreType.DMA
    slots = 16
    x, r, d, img, step = pl.pallas_call(
        functools.partial(kernel, n_cam, n_pt, tiles),
        out_shape=(share,) * 5,
        in_specs=[pl.BlockSpec(memory_space=pl.ANY)] * 9,
        out_specs=(vm,) * 5,
        scratch_shapes=[
            vmem(right_side.shape, f32), vmem(right_side.shape, f32), vmem(right_side.shape, f32),
            vmem(point_damping.shape, f32),
            vmem((18, tiles, 128), bf16), vmem((6, tiles, 128), bf16),
            vmem((tiles, 128), i32), vmem((tiles, 128), i32), pltpu.SMEM((1, 1), i32), dma((9,)),
            vmem((256, obs), bf16), vmem((128, obs), bf16),
            vmem((18, tiles, 128), f32), vmem((6, tiles, 128), f32),
            vmem((2, 9, tiles, 128), f32), vmem((384, obs), bf16), vmem((2, 384, 128), f32),
            vmem((9, tiles, 128), f32),
            vmem((2, tiles, 128), f32), vmem((2, tiles, 128), f32),
            vmem((24, 128), f32), vmem((24, 128), f32), vmem((24, 128), f32), vmem((24, 128), f32),
            vmem((24, 128), f32), vmem((24, 128), f32), vmem((7, 128), f32), vmem((16, 128), f32), vmem((1, 128), f32),
            vmem((slots, 19, 128), f32),
            vmem((slots, 7, 128), f32), vmem((slots, 7, 128), f32), vmem((slots, 7, 128), f32),
            vmem((slots, 19, 128), f32), vmem((slots, 19, 128), f32),
            vmem((slots, 16, 128), f32), vmem((slots, 16, 128), f32),
            *[dma((slots,)) for _ in range(10)],
        ],
        compiler_params=pltpu.CompilerParams(
            collective_id=0, has_side_effects=True, vmem_limit_bytes=60 << 20
        ),
        name="pcg",
    )(
        right_side, precond_diag, camera_damping, point_damping,
        camera_jacobian.reshape(18, tiles, 128), point_jacobian.reshape(6, tiles, 128),
        camera_index.reshape(tiles, 128), point_index.reshape(tiles, 128), tile_count,
    )
    return x + step * d, r - step * img


def solution(mesh):
    return jax.shard_map(
        on_device,
        mesh=mesh,
        in_specs=(
            P(None, ("cam", "pt")),
            P(None, ("cam", "pt")),
            P(None, ("cam", "pt")),
            P(None, "cam", "pt"),
            P("cam", "pt", None, None, None),
            P("cam", "pt", None, None, None),
            P("cam", "pt", None, None),
            P("cam", "pt", None, None),
            P("cam", "pt"),
        ),
        out_specs=(P(None, ("cam", "pt")), P(None, ("cam", "pt"))),
        check_vma=False,
    )
```

```python
import functools

import jax
import jax.numpy as jnp
from jax import lax
from jax.experimental import pallas as pl
from jax.experimental.pallas import tpu as pltpu
from jax.sharding import PartitionSpec as P

ITERS = 3
MESH = pl.DeviceIdType.MESH
f32, bf16, i32 = jnp.float32, jnp.bfloat16, jnp.int32

PAIRS = ((0, 0), (0, 1), (0, 2), (1, 1), (1, 2), (2, 2))
SYM = ((0, 1, 2), (1, 3, 4), (2, 4, 5))
CHUNK = 16
LANES = lax.GatherDimensionNumbers(
    offset_dims=(), collapsed_slice_dims=(1,), start_index_map=(1,),
    operand_batching_dims=(0,), start_indices_batching_dims=(0,),
)


def lane_gather(rows, lanes):
    return lax.gather(rows, lanes[..., None], LANES, (1, 1), mode=lax.GatherScatterMode.PROMISE_IN_BOUNDS)


def ring(off, size):
    return min(off, size - off)


def offsets(major, minor, near_minor):
    return sorted(
        (ring(a, major) + (0.1 if near_minor else 1) * ring(b, minor), a, b)
        for a in range(major) for b in range(minor) if a or b
    )


def split_by(offs, edges):
    groups, low = [], -1
    for edge in edges:
        part = [off for off in offs if low < off[0] <= edge]
        if part:
            groups.append(part)
        low = edge
    return groups


def kernel(
    n_cam, n_pt, tiles,
    rhs_h, pre_h, damp_h, pdamp_h, jc_h, jp_h, cidx_h, pidx_h, tcount_h,
    x_out, r_out, d_out, img_out, step_out,
    rhs, pre, damp, pdamp, jc, jp, cidx, pidx, tcount, isem,
    ohc, ohp, jcf, jpf, term, amat, acc, vals,
    u_z, u_d,
    prec_s, damp_s, x_s, r_s, d_s, img_s, pz_s, inv_s, gam_s,
    buf_a, msg_b, buf_b, buf_c, msg_d, buf_d, msg_h, buf_h,
    sa, ra, sb, rb, sc, rc, sd, rd, sh, rh,
):
    ci = lax.axis_index("cam")
    pi = lax.axis_index("pt")
    groups = tiles // 8
    pt_dims = (n_pt // 4, 4) if n_pt >= 4 else (1, n_pt)
    cam_dims = (n_cam // 2, 2)
    pt_offs = offsets(*pt_dims, False)
    cam_offs = offsets(*cam_dims, True)

    def peer_at(me, dims, off):
        major = lax.rem(lax.div(me, dims[1]) + off[1], dims[0])
        minor = lax.rem(lax.rem(me, dims[1]) + off[2], dims[1])
        return major * dims[1] + minor

    def cam_peer(off):
        return peer_at(ci, cam_dims, off)

    def pt_peer(off):
        return peer_at(pi, pt_dims, off)

    def cam_id(peer):
        return (peer, pi)

    def pt_id(peer):
        return (ci, peer)

    on_cam = (cam_offs, cam_peer, cam_id, ci)
    on_pt = (pt_offs, pt_peer, pt_id, pi)

    def ship(group, peer, src, dst, send_sem, recv_sem):
        me = group[3]
        return pltpu.make_async_remote_copy(
            src_ref=src, dst_ref=dst.at[me],
            send_sem=send_sem.at[peer], recv_sem=recv_sem.at[me],
            device_id=group[2](peer), device_id_type=MESH,
        )

    def send_all(group, src_of, dst, send_sem, recv_sem, fill=None, near=False):
        for off in group[0] if near else reversed(group[0]):
            peer = group[1](off)
            if fill is not None:
                fill(peer)
            ship(group, peer, src_of(peer), dst, send_sem, recv_sem).start()

    def wait_sent(group, src_of, dst, send_sem, recv_sem):
        for off in group[0]:
            peer = group[1](off)
            ship(group, peer, src_of(peer), dst, send_sem, recv_sem).wait_send()

    def wait_some(group, part, dst, recv_sem):
        for off in part:
            peer = group[1](off)
            pltpu.make_async_remote_copy(
                src_ref=dst.at[peer], dst_ref=dst.at[peer],
                send_sem=recv_sem.at[peer], recv_sem=recv_sem.at[peer],
                device_id=group[2](peer), device_id_type=MESH,
            ).wait_recv()

    ex_a = (on_pt, lambda peer: buf_a.at[pi], buf_a, sa, ra)
    ex_b = (on_cam, lambda peer: msg_b.at[peer], buf_b, sb, rb)
    ex_c = (on_cam, lambda peer: buf_c.at[ci], buf_c, sc, rc)
    ex_d = (on_pt, lambda peer: msg_d.at[peer], buf_d, sd, rd)
    ex_h = (on_cam, lambda peer: msg_h.at[peer], buf_h, sh, rh)

    barrier = pltpu.get_barrier_semaphore()

    def greet(group):
        for off in reversed(group[0]):
            pl.semaphore_signal(barrier, inc=1, device_id=group[2](group[1](off)), device_id_type=MESH)

    greet(on_pt)
    greet(on_cam)

    loads = [
        pltpu.make_async_copy(src, dst, isem.at[n])
        for n, (src, dst) in enumerate(
            ((rhs_h, rhs), (pre_h, pre), (tcount_h, tcount), (jp_h, jp), (pidx_h, pidx),
             (jc_h, jc), (cidx_h, cidx), (damp_h, damp), (pdamp_h, pdamp))
        )
    ]
    for load in loads:
        load.start()

    def to_share(src, dst):
        dst[...] = jnp.zeros((24, 128), f32)
        dst[0:9, :] = src[:, 0:128]
        dst[9:18, :] = src[:, 128:256]

    def from_share(value, dst):
        dst[:, 0:128] = value[0:9]
        dst[:, 128:256] = value[9:18]

    x_s[...] = jnp.zeros((24, 128), f32)
    img_s[...] = jnp.zeros((24, 128), f32)
    d_s[...] = jnp.zeros((24, 128), f32)
    pz_s[...] = jnp.zeros((7, 128), f32)
    u_d[...] = jnp.zeros_like(u_d)
    gam_s[...] = jnp.ones((1, 128), f32)

    def put_a():
        r = r_s[...]
        z = prec_s[...] * r
        buf_a[pi, 0:18, :] = z[0:18]
        buf_a[pi, 18:19, :] = jnp.sum(r * z, axis=0, keepdims=True)

    loads[0].wait()
    loads[1].wait()
    to_share(rhs, r_s)
    to_share(pre, prec_s)
    put_a()

    for load in loads[2:]:
        load.wait()
    to_share(damp, damp_s)
    live = lax.broadcasted_iota(i32, (tiles, 128), 0) < tcount[0, 0]
    for row in range(6):
        jpf[row] = jnp.where(live, jp[row].astype(f32), 0.0)
    for row in range(18):
        jcf[row] = jnp.where(live, jc[row].astype(f32), 0.0)

    def one_hot(idx, low, dst):
        iota = lax.broadcasted_iota(i32, (low, 128), 0)

        def one(t, carry):
            part = jnp.broadcast_to(idx[pl.ds(t, 1), :] & (low - 1), (low, 128))
            dst[:, pl.ds(pl.multiple_of(t * 128, 128), 128)] = jnp.where(part == iota, 1.0, 0.0).astype(bf16)
            return carry

        lax.fori_loop(0, tiles, one, 0, unroll=4)

    one_hot(pidx, 128, ohp)

    def put_term(k, at, value):
        high = value.astype(bf16).astype(f32)
        term[0, k, at, :] = high
        term[1, k, at, :] = value - high

    def scatter(nk, idx, oh, low, prepare):
        shift, high = (8, 16) if low == 256 else (7, 32)
        iota = lax.broadcasted_iota(i32, (high, 128), 0)
        rows = 2 * nk * high

        def build(c):
            for t in range(c * CHUNK, min(c * CHUNK + CHUNK, tiles)):
                if t % 8 == 0:
                    prepare(t // 8)
                m = jnp.broadcast_to(idx[t : t + 1, :] >> shift, (high, 128)) == iota
                for part in range(2):
                    for k in range(nk):
                        row = jnp.broadcast_to(term[part, k, t : t + 1, :], (high, 128))
                        at = (part * nk + k) * high
                        amat[at : at + high, t * 128 : t * 128 + 128] = jnp.where(m, row, 0.0).astype(bf16)

        chunks = pl.cdiv(tiles, CHUNK)
        build(0)
        for c in range(chunks):
            if c + 1 < chunks:
                build(c + 1)
            cols = slice(c * CHUNK * 128, min(c * CHUNK + CHUNK, tiles) * 128)
            res = lax.dot_general(
                amat[0:rows, cols], oh[:, cols], (((1,), (1,)), ((), ())), preferred_element_type=f32
            )
            for half in range(low // 128):
                mine = res[:, half * 128 : half * 128 + 128]
                if c:
                    mine = mine + acc[half, 0:rows, :]
                acc[half, 0:rows, :] = mine

    def point_rows(nk, share, half):
        at = 2 * share + half
        return acc[0, pl.ds(at, nk, stride=32), :] + acc[0, pl.ds(at + 32 * nk, nk, stride=32), :]

    def camera_rows(share, half):
        return acc[half, pl.ds(share, 9, stride=16), :] + acc[half, pl.ds(share + 144, 9, stride=16), :]

    def unroll_of(count):
        return 8

    def gather(nk, group, parts, table, row_of, recv_sem, idx, done):
        for n, part in enumerate(parts):
            wait_some(group, part, table, recv_sem)
            peers = [group[1](off) for off in part] if part else [group[3]]

            def one(g, n=n, peers=peers):
                at = pl.ds(g * 8 if isinstance(g, int) else pl.multiple_of(g * 8, 8), 8)
                own = idx[at, :]
                lanes, high = own & 127, own >> 7
                got = [vals[k, at, :] if n else jnp.zeros((8, 128), f32) for k in range(nk)]
                for peer in peers:
                    for half in range(2):
                        m = high == 2 * peer + half
                        for k in range(nk):
                            row = jnp.broadcast_to(table[peer, pl.ds(row_of(k, half), 1), :], (8, 128))
                            got[k] = jnp.where(m, lane_gather(row, lanes), got[k])
                if n == len(parts) - 1:
                    done(at, got)
                else:
                    for k in range(nk):
                        vals[k, at, :] = got[k]

            if n == len(parts) - 1:
                return one

            def step(g, carry, one=one):
                one(g)
                return carry

            lax.fori_loop(0, groups, step, 0, unroll=min(groups, unroll_of(2 * nk * len(peers))))

    for k, (a, b) in enumerate(PAIRS):
        put_term(k, slice(None), jpf[a] * jpf[b] + jpf[3 + a] * jpf[3 + b])
    acc[0] = jnp.zeros((384, 128), f32)
    iota_h = lax.broadcasted_iota(i32, (32, 128), 0)
    chunk_h = min(CHUNK, tiles)

    def curvature(c, carry):
        @pl.when(c == 1)
        def _():
            pl.semaphore_wait(barrier, (n_pt - 1) + (n_cam - 1))
            send_all(*ex_a, near=True)

        for s in range(chunk_h):
            t = c * chunk_h + s
            m = jnp.broadcast_to(pidx[pl.ds(t, 1), :] >> 7, (32, 128)) == iota_h
            for part in range(2):
                for k in range(6):
                    row = jnp.broadcast_to(term[part, k, pl.ds(t, 1), :], (32, 128))
                    at = (part * 6 + k) * 32
                    amat[at : at + 32, s * 128 : s * 128 + 128] = jnp.where(m, row, 0.0).astype(bf16)
        size = chunk_h * 128
        acc[0] += lax.dot_general(
            amat[:, 0:size], ohp[:, pl.ds(pl.multiple_of(c * size, 128), size)],
            (((1,), (1,)), ((), ())), preferred_element_type=f32,
        )
        return carry

    lax.fori_loop(0, tiles // chunk_h, curvature, 0)

    def fill_h(share):
        msg_h[share, 0:6, :] = point_rows(6, share, 0)
        msg_h[share, 8:14, :] = point_rows(6, share, 1)
        msg_h[share, 6:8, :] = jnp.zeros((2, 128), f32)
        msg_h[share, 14:16, :] = jnp.zeros((2, 128), f32)

    send_all(*ex_h, fill_h)
    fill_h(ci)
    buf_h[ci] = msg_h[ci]

    def solve_curvature():
        wait_some(on_cam, cam_offs, buf_h, rh)
        h = buf_h[0]
        for share in range(1, n_cam):
            h = h + buf_h[share]
        for half in range(2):
            lanes = slice(half * 128, half * 128 + 128)
            e = [h[8 * half + k : 8 * half + k + 1, :] for k in range(6)]
            e[0] = e[0] + pdamp[0, :, lanes]
            e[3] = e[3] + pdamp[1, :, lanes]
            e[5] = e[5] + pdamp[2, :, lanes]
            a1 = e[3] * e[5] - e[4] * e[4]
            a2 = e[2] * e[4] - e[1] * e[5]
            a3 = e[1] * e[4] - e[2] * e[3]
            a4 = e[0] * e[5] - e[2] * e[2]
            a5 = e[1] * e[2] - e[0] * e[4]
            a6 = e[0] * e[3] - e[1] * e[1]
            det = e[0] * a1 + e[1] * a2 + e[2] * a3
            for k, value in enumerate((a1, a2, a3, a4, a5, a6)):
                inv_s[8 * half + k : 8 * half + k + 1, :] = value / det
        wait_sent(*ex_h)

    def iteration(it, carry):
        def put_u(at, v):
            u0 = sum(jcf[k, at, :] * v[k] for k in range(9))
            u1 = sum(jcf[9 + k, at, :] * v[k] for k in range(9))
            u_z[0, at, :] = u0
            u_z[1, at, :] = u1
            for k in range(3):
                put_term(k, at, jpf[k, at, :] * u0 + jpf[3 + k, at, :] * u1)

        prepare = gather(9, on_pt, [[], *split_by(pt_offs, (1, 2, 3, 9))], buf_a, lambda k, half: 9 * half + k, ra, cidx, put_u)
        grow = buf_a[0, 18:19, :]
        for share in range(1, n_pt):
            grow = grow + buf_a[share, 18:19, :]

        scatter(3, pidx, ohp, 128, prepare)

        def fill_b(share):
            msg_b[share, 0:3, :] = point_rows(3, share, 0)
            msg_b[share, 4:7, :] = point_rows(3, share, 1)
            msg_b[share, 3:4, :] = grow

        send_all(*ex_b, fill_b)
        fill_b(ci)
        buf_b[ci] = msg_b[ci]
        wait_sent(*ex_a)

        @pl.when(it == 0)
        def _():
            one_hot(cidx, 256, ohc)
            solve_curvature()

        wait_some(on_cam, cam_offs, buf_b, rb)
        pz = buf_b[0]
        for share in range(1, n_cam):
            pz = pz + buf_b[share]
        energy = jnp.broadcast_to(jnp.sum(pz[3:4, :], axis=1, keepdims=True), (1, 128))
        beta = jnp.where(it == 0, 0.0, energy / gam_s[...])
        gam_s[...] = energy
        pd = pz + beta * pz_s[...]
        pz_s[...] = pd
        d = prec_s[...] * r_s[...] + beta * d_s[...]
        d_s[...] = d
        part = jnp.sum(damp_s[...] * d * d, axis=0, keepdims=True)
        squares = jnp.zeros((8, 128), f32)
        for g in range(groups):
            for comp in range(2):
                u = u_z[comp, 8 * g : 8 * g + 8, :] + beta * u_d[comp, 8 * g : 8 * g + 8, :]
                u_d[comp, 8 * g : 8 * g + 8, :] = u
                squares = squares + u * u
        part = part + jnp.sum(squares, axis=0, keepdims=True)
        for half in range(2):
            v = [pd[4 * half + k : 4 * half + k + 1, :] for k in range(3)]
            m = [inv_s[8 * half + k : 8 * half + k + 1, :] for k in range(6)]
            for row in range(3):
                at = 4 * half + row
                q = sum(m[SYM[row][col]] * v[col] for col in range(3))
                buf_c[ci, at : at + 1, :] = q
                part = part - q * v[row]
        buf_c[ci, 3:4, :] = part
        send_all(*ex_c)
        wait_sent(*ex_b)

        def put_w(at, q):
            u0, u1 = u_d[0, at, :], u_d[1, at, :]
            w0 = u0 - sum(jpf[k, at, :] * q[k] for k in range(3))
            w1 = u1 - sum(jpf[3 + k, at, :] * q[k] for k in range(3))
            for k in range(9):
                put_term(k, at, jcf[k, at, :] * w0 + jcf[9 + k, at, :] * w1)

        prepare = gather(3, on_cam, [[], *split_by(cam_offs, (0.5, 2.5, 3.5, 9))], buf_c, lambda k, half: 4 * half + k, rc, pidx, put_w)
        dots = buf_c[0, 3:4, :]
        for share in range(1, n_cam):
            dots = dots + buf_c[share, 3:4, :]

        scatter(9, cidx, ohc, 256, prepare)

        def fill_d(share):
            msg_d[share, 0:9, :] = camera_rows(share, 0)
            msg_d[share, 9:18, :] = camera_rows(share, 1)
            msg_d[share, 18:19, :] = dots

        send_all(*ex_d, fill_d)
        fill_d(pi)
        buf_d[pi] = msg_d[pi]
        wait_sent(*ex_c)
        wait_some(on_pt, pt_offs, buf_d, rd)
        img = buf_d[0]
        for share in range(1, n_pt):
            img = img + buf_d[share]
        step_len = energy / jnp.broadcast_to(jnp.sum(img[18:19, :], axis=1, keepdims=True), (1, 128))
        img_s[0:18, :] = img[0:18]
        img = img_s[...] + damp_s[...] * d

        @pl.when(it == ITERS - 1)
        def _():
            from_share(img, img_out)
            from_share(d, d_out)
            from_share(x_s[...], x_out)
            from_share(r_s[...], r_out)
            step_out[...] = jnp.broadcast_to(step_len[:, 0:1], step_out.shape)

        @pl.when(it < ITERS - 1)
        def _():
            x_s[...] = x_s[...] + step_len * d
            r_s[...] = r_s[...] - step_len * img
            put_a()
            send_all(*ex_a, near=True)

        wait_sent(*ex_d)
        return carry

    lax.fori_loop(0, ITERS, iteration, 0)


def on_device(
    right_side, precond_diag, camera_damping, point_damping,
    camera_jacobian, point_jacobian, camera_index, point_index, tile_count,
):
    n_cam, n_pt = lax.axis_size("cam"), lax.axis_size("pt")
    tiles = camera_index.shape[2]
    obs = tiles * 128
    vm = pl.BlockSpec(memory_space=pltpu.VMEM)
    share = jax.ShapeDtypeStruct(right_side.shape, f32)
    vmem = pltpu.VMEM
    dma = pltpu.SemaphoreType.DMA
    slots = 16
    x, r, d, img, step = pl.pallas_call(
        functools.partial(kernel, n_cam, n_pt, tiles),
        out_shape=(share,) * 5,
        in_specs=[pl.BlockSpec(memory_space=pl.ANY)] * 9,
        out_specs=(vm,) * 5,
        scratch_shapes=[
            vmem(right_side.shape, f32), vmem(right_side.shape, f32), vmem(right_side.shape, f32),
            vmem(point_damping.shape, f32),
            vmem((18, tiles, 128), bf16), vmem((6, tiles, 128), bf16),
            vmem((tiles, 128), i32), vmem((tiles, 128), i32), pltpu.SMEM((1, 1), i32), dma((9,)),
            vmem((256, obs), bf16), vmem((128, obs), bf16),
            vmem((18, tiles, 128), f32), vmem((6, tiles, 128), f32),
            vmem((2, 9, tiles, 128), f32), vmem((384, obs), bf16), vmem((2, 384, 128), f32),
            vmem((9, tiles, 128), f32),
            vmem((2, tiles, 128), f32), vmem((2, tiles, 128), f32),
            vmem((24, 128), f32), vmem((24, 128), f32), vmem((24, 128), f32), vmem((24, 128), f32),
            vmem((24, 128), f32), vmem((24, 128), f32), vmem((7, 128), f32), vmem((16, 128), f32), vmem((1, 128), f32),
            vmem((slots, 19, 128), f32),
            vmem((slots, 7, 128), f32), vmem((slots, 7, 128), f32), vmem((slots, 7, 128), f32),
            vmem((slots, 19, 128), f32), vmem((slots, 19, 128), f32),
            vmem((slots, 16, 128), f32), vmem((slots, 16, 128), f32),
            *[dma((slots,)) for _ in range(10)],
        ],
        compiler_params=pltpu.CompilerParams(
            collective_id=0, has_side_effects=True, vmem_limit_bytes=60 << 20
        ),
        name="pcg",
    )(
        right_side, precond_diag, camera_damping, point_damping,
        camera_jacobian.reshape(18, tiles, 128), point_jacobian.reshape(6, tiles, 128),
        camera_index.reshape(tiles, 128), point_index.reshape(tiles, 128), tile_count,
    )
    return x + step * d, r - step * img


def solution(mesh):
    return jax.shard_map(
        on_device,
        mesh=mesh,
        in_specs=(
            P(None, ("cam", "pt")),
            P(None, ("cam", "pt")),
            P(None, ("cam", "pt")),
            P(None, "cam", "pt"),
            P("cam", "pt", None, None, None),
            P("cam", "pt", None, None, None),
            P("cam", "pt", None, None),
            P("cam", "pt", None, None),
            P("cam", "pt"),
        ),
        out_specs=(P(None, ("cam", "pt")), P(None, ("cam", "pt"))),
        check_vma=False,
    )
```

```python
import functools

import jax
import jax.numpy as jnp
from jax import lax
from jax.experimental import pallas as pl
from jax.experimental.pallas import tpu as pltpu
from jax.sharding import PartitionSpec as P

ITERS = 3
MESH = pl.DeviceIdType.MESH
f32, bf16, i32 = jnp.float32, jnp.bfloat16, jnp.int32

PAIRS = ((0, 0), (0, 1), (0, 2), (1, 1), (1, 2), (2, 2))
SYM = ((0, 1, 2), (1, 3, 4), (2, 4, 5))
CHUNK = 16
LANES = lax.GatherDimensionNumbers(
    offset_dims=(), collapsed_slice_dims=(1,), start_index_map=(1,),
    operand_batching_dims=(0,), start_indices_batching_dims=(0,),
)


def lane_gather(rows, lanes):
    return lax.gather(rows, lanes[..., None], LANES, (1, 1), mode=lax.GatherScatterMode.PROMISE_IN_BOUNDS)


def ring(off, size):
    return min(off, size - off)


def offsets(major, minor, near_minor):
    return sorted(
        (ring(a, major) + (0.1 if near_minor else 1) * ring(b, minor), a, b)
        for a in range(major) for b in range(minor) if a or b
    )


def split_by(offs, edges):
    groups, low = [], -1
    for edge in edges:
        part = [off for off in offs if low < off[0] <= edge]
        if part:
            groups.append(part)
        low = edge
    return groups


def kernel(
    n_cam, n_pt, tiles,
    rhs_h, pre_h, damp_h, pdamp_h, jc_h, jp_h, cidx_h, pidx_h, tcount_h,
    out,
    rhs, pre, damp, pdamp, jc, jp, cidx, pidx, tcount, isem,
    ohc, ohp, jcf, jpf, term, amat, acc, vals,
    u_z, u_d,
    prec_s, damp_s, x_s, r_s, d_s, img_s, pz_s, inv_s, gam_s,
    buf_a, msg_b, buf_b, buf_c, msg_d, buf_d, msg_h, buf_h,
    sa, ra, sb, rb, sc, rc, sd, rd, sh, rh,
):
    ci = lax.axis_index("cam")
    pi = lax.axis_index("pt")
    groups = tiles // 8
    pt_dims = (n_pt // 4, 4) if n_pt >= 4 else (1, n_pt)
    cam_dims = (n_cam // 2, 2)
    pt_offs = offsets(*pt_dims, False)
    cam_offs = offsets(*cam_dims, True)

    def peer_at(me, dims, off):
        major = lax.rem(lax.div(me, dims[1]) + off[1], dims[0])
        minor = lax.rem(lax.rem(me, dims[1]) + off[2], dims[1])
        return major * dims[1] + minor

    def cam_peer(off):
        return peer_at(ci, cam_dims, off)

    def pt_peer(off):
        return peer_at(pi, pt_dims, off)

    def cam_id(peer):
        return (peer, pi)

    def pt_id(peer):
        return (ci, peer)

    on_cam = (cam_offs, cam_peer, cam_id, ci)
    on_pt = (pt_offs, pt_peer, pt_id, pi)

    def ship(group, peer, src, dst, send_sem, recv_sem):
        me = group[3]
        return pltpu.make_async_remote_copy(
            src_ref=src, dst_ref=dst.at[me],
            send_sem=send_sem.at[peer], recv_sem=recv_sem.at[me],
            device_id=group[2](peer), device_id_type=MESH,
        )

    def send_all(group, src_of, dst, send_sem, recv_sem, fill=None, near=False):
        for off in group[0] if near else reversed(group[0]):
            peer = group[1](off)
            if fill is not None:
                fill(peer)
            ship(group, peer, src_of(peer), dst, send_sem, recv_sem).start()

    def wait_sent(group, src_of, dst, send_sem, recv_sem):
        for off in group[0]:
            peer = group[1](off)
            ship(group, peer, src_of(peer), dst, send_sem, recv_sem).wait_send()

    def wait_some(group, part, dst, recv_sem):
        for off in part:
            peer = group[1](off)
            pltpu.make_async_remote_copy(
                src_ref=dst.at[peer], dst_ref=dst.at[peer],
                send_sem=recv_sem.at[peer], recv_sem=recv_sem.at[peer],
                device_id=group[2](peer), device_id_type=MESH,
            ).wait_recv()

    ex_a = (on_pt, lambda peer: buf_a.at[pi], buf_a, sa, ra)
    ex_b = (on_cam, lambda peer: msg_b.at[peer], buf_b, sb, rb)
    ex_c = (on_cam, lambda peer: buf_c.at[ci], buf_c, sc, rc)
    ex_d = (on_pt, lambda peer: msg_d.at[peer], buf_d, sd, rd)
    ex_h = (on_cam, lambda peer: msg_h.at[peer], buf_h, sh, rh)

    barrier = pltpu.get_barrier_semaphore()

    def greet(group):
        for off in reversed(group[0]):
            pl.semaphore_signal(barrier, inc=1, device_id=group[2](group[1](off)), device_id_type=MESH)

    greet(on_pt)
    greet(on_cam)

    loads = [
        pltpu.make_async_copy(src, dst, isem.at[n])
        for n, (src, dst) in enumerate(
            ((rhs_h, rhs), (pre_h, pre), (tcount_h, tcount), (jp_h, jp), (pidx_h, pidx),
             (jc_h, jc), (cidx_h, cidx), (damp_h, damp), (pdamp_h, pdamp))
        )
    ]
    for load in loads:
        load.start()

    def to_share(src, dst):
        dst[...] = jnp.zeros((24, 128), f32)
        dst[0:9, :] = src[:, 0:128]
        dst[9:18, :] = src[:, 128:256]

    def from_share(value, n):
        out[:, n * 256 : n * 256 + 128] = value[0:9]
        out[:, n * 256 + 128 : n * 256 + 256] = value[9:18]

    x_s[...] = jnp.zeros((24, 128), f32)
    img_s[...] = jnp.zeros((24, 128), f32)
    d_s[...] = jnp.zeros((24, 128), f32)
    pz_s[...] = jnp.zeros((7, 128), f32)
    u_d[...] = jnp.zeros_like(u_d)
    gam_s[...] = jnp.ones((1, 128), f32)

    def put_a():
        r = r_s[...]
        z = prec_s[...] * r
        buf_a[pi, 0:18, :] = z[0:18]
        buf_a[pi, 18:19, :] = jnp.sum(r * z, axis=0, keepdims=True)

    loads[0].wait()
    loads[1].wait()
    to_share(rhs, r_s)
    to_share(pre, prec_s)
    put_a()

    for load in loads[2:]:
        load.wait()
    to_share(damp, damp_s)
    live = lax.broadcasted_iota(i32, (tiles, 128), 0) < tcount[0, 0]
    for row in range(6):
        jpf[row] = jnp.where(live, jp[row].astype(f32), 0.0)
    for row in range(18):
        jcf[row] = jnp.where(live, jc[row].astype(f32), 0.0)

    def one_hot(idx, low, dst):
        iota = lax.broadcasted_iota(i32, (low, 128), 0)

        def one(t, carry):
            part = jnp.broadcast_to(idx[pl.ds(t, 1), :] & (low - 1), (low, 128))
            dst[:, pl.ds(pl.multiple_of(t * 128, 128), 128)] = jnp.where(part == iota, 1.0, 0.0).astype(bf16)
            return carry

        lax.fori_loop(0, tiles, one, 0, unroll=4)

    one_hot(pidx, 128, ohp)

    def put_term(k, at, value):
        high = value.astype(bf16).astype(f32)
        term[0, k, at, :] = high
        term[1, k, at, :] = value - high

    def scatter(nk, idx, oh, low, prepare):
        shift, high = (8, 16) if low == 256 else (7, 32)
        iota = lax.broadcasted_iota(i32, (high, 128), 0)
        rows = 2 * nk * high

        def build(c):
            for t in range(c * CHUNK, min(c * CHUNK + CHUNK, tiles)):
                if t % 8 == 0:
                    prepare(t // 8)
                m = jnp.broadcast_to(idx[t : t + 1, :] >> shift, (high, 128)) == iota
                for part in range(2):
                    for k in range(nk):
                        row = jnp.broadcast_to(term[part, k, t : t + 1, :], (high, 128))
                        at = (part * nk + k) * high
                        amat[at : at + high, t * 128 : t * 128 + 128] = jnp.where(m, row, 0.0).astype(bf16)

        chunks = pl.cdiv(tiles, CHUNK)
        build(0)
        for c in range(chunks):
            if c + 1 < chunks:
                build(c + 1)
            cols = slice(c * CHUNK * 128, min(c * CHUNK + CHUNK, tiles) * 128)
            res = lax.dot_general(
                amat[0:rows, cols], oh[:, cols], (((1,), (1,)), ((), ())), preferred_element_type=f32
            )
            for half in range(low // 128):
                mine = res[:, half * 128 : half * 128 + 128]
                if c:
                    mine = mine + acc[half, 0:rows, :]
                acc[half, 0:rows, :] = mine

    def point_rows(nk, share, half):
        at = 2 * share + half
        return acc[0, pl.ds(at, nk, stride=32), :] + acc[0, pl.ds(at + 32 * nk, nk, stride=32), :]

    def camera_rows(share, half):
        return acc[half, pl.ds(share, 9, stride=16), :] + acc[half, pl.ds(share + 144, 9, stride=16), :]

    def unroll_of(count):
        return 8

    def gather(nk, group, parts, table, row_of, recv_sem, idx, done):
        for n, part in enumerate(parts):
            wait_some(group, part, table, recv_sem)
            peers = [group[1](off) for off in part] if part else [group[3]]

            def one(g, n=n, peers=peers):
                at = pl.ds(g * 8 if isinstance(g, int) else pl.multiple_of(g * 8, 8), 8)
                own = idx[at, :]
                lanes, high = own & 127, own >> 7
                got = [vals[k, at, :] if n else jnp.zeros((8, 128), f32) for k in range(nk)]
                for peer in peers:
                    for half in range(2):
                        m = high == 2 * peer + half
                        for k in range(nk):
                            row = jnp.broadcast_to(table[peer, pl.ds(row_of(k, half), 1), :], (8, 128))
                            got[k] = jnp.where(m, lane_gather(row, lanes), got[k])
                if n == len(parts) - 1:
                    done(at, got)
                else:
                    for k in range(nk):
                        vals[k, at, :] = got[k]

            if n == len(parts) - 1:
                return one

            def step(g, carry, one=one):
                one(g)
                return carry

            lax.fori_loop(0, groups, step, 0, unroll=min(groups, unroll_of(2 * nk * len(peers))))

    for k, (a, b) in enumerate(PAIRS):
        put_term(k, slice(None), jpf[a] * jpf[b] + jpf[3 + a] * jpf[3 + b])
    acc[0] = jnp.zeros((384, 128), f32)
    iota_h = lax.broadcasted_iota(i32, (32, 128), 0)
    chunk_h = min(CHUNK, tiles)

    def curvature(c, carry):
        @pl.when(c == 1)
        def _():
            pl.semaphore_wait(barrier, (n_pt - 1) + (n_cam - 1))
            send_all(*ex_a, near=True)

        for s in range(chunk_h):
            t = c * chunk_h + s
            m = jnp.broadcast_to(pidx[pl.ds(t, 1), :] >> 7, (32, 128)) == iota_h
            for part in range(2):
                for k in range(6):
                    row = jnp.broadcast_to(term[part, k, pl.ds(t, 1), :], (32, 128))
                    at = (part * 6 + k) * 32
                    amat[at : at + 32, s * 128 : s * 128 + 128] = jnp.where(m, row, 0.0).astype(bf16)
        size = chunk_h * 128
        acc[0] += lax.dot_general(
            amat[:, 0:size], ohp[:, pl.ds(pl.multiple_of(c * size, 128), size)],
            (((1,), (1,)), ((), ())), preferred_element_type=f32,
        )
        return carry

    lax.fori_loop(0, tiles // chunk_h, curvature, 0)

    def fill_h(share):
        msg_h[share, 0:6, :] = point_rows(6, share, 0)
        msg_h[share, 8:14, :] = point_rows(6, share, 1)
        msg_h[share, 6:8, :] = jnp.zeros((2, 128), f32)
        msg_h[share, 14:16, :] = jnp.zeros((2, 128), f32)

    send_all(*ex_h, fill_h)
    fill_h(ci)
    buf_h[ci] = msg_h[ci]

    def solve_curvature():
        wait_some(on_cam, cam_offs, buf_h, rh)
        h = buf_h[0]
        for share in range(1, n_cam):
            h = h + buf_h[share]
        for half in range(2):
            lanes = slice(half * 128, half * 128 + 128)
            e = [h[8 * half + k : 8 * half + k + 1, :] for k in range(6)]
            e[0] = e[0] + pdamp[0, :, lanes]
            e[3] = e[3] + pdamp[1, :, lanes]
            e[5] = e[5] + pdamp[2, :, lanes]
            a1 = e[3] * e[5] - e[4] * e[4]
            a2 = e[2] * e[4] - e[1] * e[5]
            a3 = e[1] * e[4] - e[2] * e[3]
            a4 = e[0] * e[5] - e[2] * e[2]
            a5 = e[1] * e[2] - e[0] * e[4]
            a6 = e[0] * e[3] - e[1] * e[1]
            det = e[0] * a1 + e[1] * a2 + e[2] * a3
            for k, value in enumerate((a1, a2, a3, a4, a5, a6)):
                inv_s[8 * half + k : 8 * half + k + 1, :] = value / det
        wait_sent(*ex_h)

    def iteration(it, carry):
        def put_u(at, v):
            u0 = sum(jcf[k, at, :] * v[k] for k in range(9))
            u1 = sum(jcf[9 + k, at, :] * v[k] for k in range(9))
            u_z[0, at, :] = u0
            u_z[1, at, :] = u1
            for k in range(3):
                put_term(k, at, jpf[k, at, :] * u0 + jpf[3 + k, at, :] * u1)

        prepare = gather(9, on_pt, [[], *split_by(pt_offs, (1, 2, 3, 9))], buf_a, lambda k, half: 9 * half + k, ra, cidx, put_u)
        grow = buf_a[0, 18:19, :]
        for share in range(1, n_pt):
            grow = grow + buf_a[share, 18:19, :]

        scatter(3, pidx, ohp, 128, prepare)

        def fill_b(share):
            msg_b[share, 0:3, :] = point_rows(3, share, 0)
            msg_b[share, 4:7, :] = point_rows(3, share, 1)
            msg_b[share, 3:4, :] = grow

        send_all(*ex_b, fill_b)
        fill_b(ci)
        buf_b[ci] = msg_b[ci]
        wait_sent(*ex_a)

        @pl.when(it == 0)
        def _():
            one_hot(cidx, 256, ohc)
            solve_curvature()

        z, old = prec_s[...] * r_s[...], d_s[...]
        sq = [damp_s[...] * z * z, damp_s[...] * z * old, damp_s[...] * old * old]
        sq = [v[0:8] + v[8:16] + v[16:24] for v in sq]
        for g in range(groups):
            for comp in range(2):
                new, past = u_z[comp, 8 * g : 8 * g + 8, :], u_d[comp, 8 * g : 8 * g + 8, :]
                sq = [sq[0] + new * new, sq[1] + new * past, sq[2] + past * past]
        sq = [jnp.sum(v, axis=0, keepdims=True) for v in sq]

        wait_some(on_cam, cam_offs, buf_b, rb)
        pz = buf_b[0]
        for share in range(1, n_cam):
            pz = pz + buf_b[share]
        energy = jnp.broadcast_to(jnp.sum(pz[3:4, :], axis=1, keepdims=True), (1, 128))
        beta = jnp.where(it == 0, 0.0, energy / gam_s[...])
        gam_s[...] = energy
        pd = pz + beta * pz_s[...]
        pz_s[...] = pd
        part = sq[0] + beta * (2.0 * sq[1] + beta * sq[2])
        for half in range(2):
            v = [pd[4 * half + k : 4 * half + k + 1, :] for k in range(3)]
            m = [inv_s[8 * half + k : 8 * half + k + 1, :] for k in range(6)]
            for row in range(3):
                at = 4 * half + row
                q = sum(m[SYM[row][col]] * v[col] for col in range(3))
                buf_c[ci, at : at + 1, :] = q
                part = part - q * v[row]
        buf_c[ci, 3:4, :] = part
        send_all(*ex_c)
        d = z + beta * old
        d_s[...] = d
        u_d[...] = u_z[...] + beta.reshape(1, 1, 128) * u_d[...]
        wait_sent(*ex_b)

        def put_w(at, q):
            u0, u1 = u_d[0, at, :], u_d[1, at, :]
            w0 = u0 - sum(jpf[k, at, :] * q[k] for k in range(3))
            w1 = u1 - sum(jpf[3 + k, at, :] * q[k] for k in range(3))
            for k in range(9):
                put_term(k, at, jcf[k, at, :] * w0 + jcf[9 + k, at, :] * w1)

        prepare = gather(3, on_cam, [[], *split_by(cam_offs, (0.5, 2.5, 3.5, 9))], buf_c, lambda k, half: 4 * half + k, rc, pidx, put_w)
        dots = buf_c[0, 3:4, :]
        for share in range(1, n_cam):
            dots = dots + buf_c[share, 3:4, :]

        scatter(9, cidx, ohc, 256, prepare)

        def fill_d(share):
            msg_d[share, 0:9, :] = camera_rows(share, 0)
            msg_d[share, 9:18, :] = camera_rows(share, 1)
            msg_d[share, 18:19, :] = dots

        send_all(*ex_d, fill_d)
        fill_d(pi)
        buf_d[pi] = msg_d[pi]
        wait_sent(*ex_c)
        wait_some(on_pt, pt_offs, buf_d, rd)
        img = buf_d[0]
        for share in range(1, n_pt):
            img = img + buf_d[share]
        step_len = energy / jnp.broadcast_to(jnp.sum(img[18:19, :], axis=1, keepdims=True), (1, 128))
        img_s[0:18, :] = img[0:18]
        img = img_s[...] + damp_s[...] * d

        @pl.when(it == ITERS - 1)
        def _():
            from_share(x_s[...], 0)
            from_share(r_s[...], 1)
            from_share(d, 2)
            from_share(img, 3)
            out[:, 1024:1280] = jnp.broadcast_to(step_len[:, 0:1], (9, 256))

        @pl.when(it < ITERS - 1)
        def _():
            x_s[...] = x_s[...] + step_len * d
            r_s[...] = r_s[...] - step_len * img
            put_a()
            send_all(*ex_a, near=True)

        wait_sent(*ex_d)
        return carry

    lax.fori_loop(0, ITERS, iteration, 0)


def on_device(
    right_side, precond_diag, camera_damping, point_damping,
    camera_jacobian, point_jacobian, camera_index, point_index, tile_count,
):
    n_cam, n_pt = lax.axis_size("cam"), lax.axis_size("pt")
    tiles = camera_index.shape[2]
    obs = tiles * 128
    vm = pl.BlockSpec(memory_space=pltpu.VMEM)
    vmem = pltpu.VMEM
    dma = pltpu.SemaphoreType.DMA
    slots = 16
    out = pl.pallas_call(
        functools.partial(kernel, n_cam, n_pt, tiles),
        out_shape=jax.ShapeDtypeStruct((9, 5 * 256), f32),
        in_specs=[pl.BlockSpec(memory_space=pl.ANY)] * 9,
        out_specs=vm,
        scratch_shapes=[
            vmem(right_side.shape, f32), vmem(right_side.shape, f32), vmem(right_side.shape, f32),
            vmem(point_damping.shape, f32),
            vmem((18, tiles, 128), bf16), vmem((6, tiles, 128), bf16),
            vmem((tiles, 128), i32), vmem((tiles, 128), i32), pltpu.SMEM((1, 1), i32), dma((9,)),
            vmem((256, obs), bf16), vmem((128, obs), bf16),
            vmem((18, tiles, 128), f32), vmem((6, tiles, 128), f32),
            vmem((2, 9, tiles, 128), f32), vmem((384, obs), bf16), vmem((2, 384, 128), f32),
            vmem((9, tiles, 128), f32),
            vmem((2, tiles, 128), f32), vmem((2, tiles, 128), f32),
            vmem((24, 128), f32), vmem((24, 128), f32), vmem((24, 128), f32), vmem((24, 128), f32),
            vmem((24, 128), f32), vmem((24, 128), f32), vmem((7, 128), f32), vmem((16, 128), f32), vmem((1, 128), f32),
            vmem((slots, 19, 128), f32),
            vmem((slots, 7, 128), f32), vmem((slots, 7, 128), f32), vmem((slots, 7, 128), f32),
            vmem((slots, 19, 128), f32), vmem((slots, 19, 128), f32),
            vmem((slots, 16, 128), f32), vmem((slots, 16, 128), f32),
            *[dma((slots,)) for _ in range(10)],
        ],
        compiler_params=pltpu.CompilerParams(
            collective_id=0, has_side_effects=True, vmem_limit_bytes=60 << 20
        ),
        name="pcg",
    )(
        right_side, precond_diag, camera_damping, point_damping,
        camera_jacobian.reshape(18, tiles, 128), point_jacobian.reshape(6, tiles, 128),
        camera_index.reshape(tiles, 128), point_index.reshape(tiles, 128), tile_count,
    )
    x, r, d, img, step = (out[:, 256 * n : 256 * n + 256] for n in range(5))
    return x + step * d, r - step * img


def solution(mesh):
    return jax.shard_map(
        on_device,
        mesh=mesh,
        in_specs=(
            P(None, ("cam", "pt")),
            P(None, ("cam", "pt")),
            P(None, ("cam", "pt")),
            P(None, "cam", "pt"),
            P("cam", "pt", None, None, None),
            P("cam", "pt", None, None, None),
            P("cam", "pt", None, None),
            P("cam", "pt", None, None),
            P("cam", "pt"),
        ),
        out_specs=(P(None, ("cam", "pt")), P(None, ("cam", "pt"))),
        check_vma=False,
    )
```
